32 devices in a mesh: gx: 2 (over y), gy: 4 (over x, core), gz: 4 (over z).
Axes of the slice: x: 2, y: 2, z: 4, core: 2. Of those that a mesh axis runs over, the one named last changes fastest.
Arguments:
- fill_mask: int32 [32, 32, 512], P('gx', 'gy', 'gz'), may hold values from 0 to 1, as said below
- membrane_flags: int32 [32, 32, 512], P('gx', 'gy', 'gz'), may hold values from 0 to 1, as said below
- smear: float32 [32, 32, 512], P('gx', 'gy', 'gz'), may hold values from 0 to 1, as said below
- velocity: float32 [3, 32, 32, 512], P(None, 'gx', 'gy', 'gz'), may hold values from -6 to 6
Outputs:
- velocity_out: float32 [3, 32, 32, 512], P(None, 'gx', 'gy', 'gz')
- fraction_out: float32 [32, 32, 512], P('gx', 'gy', 'gz')
The draws below stay inside these ranges and needn't reach their ends.
Inputs may be any that keep to these rules, and one draw needn't show every extreme that they name: In every column along the height, fill_mask is 1 below a surface height and 0 above it; the surface lies strictly inside the tank. membrane_flags is nonzero only on the four planes across the length at positions 4 + k * 8. smear is nonzero only on the two cells of each column next to its liquid surface.
All inputs are finite; a program needn't handle non-finite values.
Results may differ from the reference program's by a relative error of at most 0.0003.
Values sent between devices are 32-bit elements; how exact they have to be, the bound alone decides.
A program may use at most 128 MiB of HBM per device.

```python
import jax
import jax.numpy as jnp

LEVELS = 4
COARSE_SWEEPS = 8
NX = 32
NY = 32
NZ = 512


def tent(position, period):
    folded = position % period
    return 2 * jnp.minimum(folded, period - folded) - period // 2


def surface_height(key):
    key = jax.random.fold_in(key, 101)
    keys = jax.random.split(key, 5)
    xs = jnp.arange(NX, dtype=jnp.int32)[:, None]
    ys = jnp.arange(NY, dtype=jnp.int32)[None, :]
    phase_x = jax.random.randint(keys[0], (), 0, NX)
    phase_y = jax.random.randint(keys[1], (), 0, NY)
    amp_x = jax.random.randint(keys[2], (), NZ // 16, NZ // 6 + 1)
    amp_y = jax.random.randint(keys[3], (), 0, NZ // 12 + 1)
    wave = amp_x * tent(xs + phase_x, NX) // (NX // 2) + amp_y * tent(2 * ys + phase_y, NY) // max(NY // 2, 1)
    jitter = jax.random.randint(keys[4], (NX, NY), -1, 2)
    return (NZ // 2 + wave + jitter).astype(jnp.int32)


def draw_fill_mask(key, part):
    height = surface_height(key)
    heights = jnp.arange(NZ, dtype=jnp.int32)[None, None, :]
    return (heights < height[:, :, None]).astype(jnp.int32)


def draw_membrane_flags(key, part):
    key = jax.random.fold_in(key, 2)
    xs = jnp.arange(NX, dtype=jnp.int32)[:, None, None]
    plane = xs % (NX // 4) == NX // 8
    holes = jax.random.randint(key, (NX, NY, NZ), 0, 4) > 0
    return (plane & holes).astype(jnp.int32)


def draw_smear(key, part):
    height = surface_height(key)
    key = jax.random.fold_in(key, 3)
    heights = jnp.arange(NZ, dtype=jnp.int32)[None, None, :]
    near = (heights >= height[:, :, None] - 1) & (heights <= height[:, :, None])
    values = jax.random.uniform(key, (NX, NY, NZ), jnp.float32, 0.0, 1.0)
    return jnp.where(near, values, 0.0).astype(jnp.float32)


def wave_along(length, phase, view):
    positions = jnp.arange(length, dtype=jnp.float32) + phase
    return jnp.sin(positions * (2.0 * 3.141592653589793 / 32.0)).reshape(view)


def draw_velocity(key, part):
    key = jax.random.fold_in(key, 4)
    keys = jax.random.split(key, 2)
    shape = (3, NX, NY, NZ)
    noise = jnp.clip(jax.random.normal(keys[0], shape, jnp.float32), -4.0, 4.0)
    amplitude = 1.5
    phases = jax.random.uniform(keys[1], (3,), jnp.float32, 0.0, 32.0)
    full = (NX, NY, NZ)
    smooth = jnp.stack([jnp.broadcast_to(wave_along(NX, phases[0], (NX, 1, 1)), full), jnp.broadcast_to(wave_along(NY, phases[1], (1, NY, 1)), full), jnp.broadcast_to(wave_along(NZ, phases[2], (1, 1, NZ)), full)])
    return (noise + amplitude * smooth).astype(jnp.float32)


def setup_inputs(seed: int = 0) -> dict:
    streams_of = jax.random.split(jax.random.key(seed), 5)
    fill_mask = draw_fill_mask(jax.random.fold_in(streams_of[4], 71), 0)
    membrane_flags = draw_membrane_flags(jax.random.fold_in(streams_of[4], 71), 0)
    smear = draw_smear(jax.random.fold_in(streams_of[4], 71), 0)
    velocity = draw_velocity(jax.random.fold_in(streams_of[4], 71), 0)
    return {"fill_mask": fill_mask, "membrane_flags": membrane_flags, "smear": smear, "velocity": velocity}


RHO_LIQUID = 1000.0
RHO_GAS = 1.0
MEMBRANE_DROP = 49.0
SIGMA_SHIFT = 0.1
OMEGA = 0.8
TIME_STEP = 0.2


def phase_fields(fill_mask, membrane_flags, smear):
    filled = fill_mask.astype(jnp.float32)
    walled = membrane_flags.astype(jnp.float32)
    fraction = filled * (1.0 - 0.4 * smear) + (1.0 - filled) * (0.4 * smear)
    density = RHO_GAS + (RHO_LIQUID - RHO_GAS) * fraction
    conductance = 1.0 / (density * (1.0 + MEMBRANE_DROP * walled))
    return fraction, conductance


def harmonic(lower_value, upper_value):
    return 2.0 * lower_value * upper_value / (lower_value + upper_value)


def fine_tables(padded):
    center = padded[1:-1, 1:-1, 1:-1]
    upper_faces = [harmonic(center, padded[2:, 1:-1, 1:-1]), harmonic(center, padded[1:-1, 2:, 1:-1]), harmonic(center, padded[1:-1, 1:-1, 2:])]
    lower_faces = [harmonic(padded[:-2, 1:-1, 1:-1], center), harmonic(padded[1:-1, :-2, 1:-1], center), harmonic(padded[1:-1, 1:-1, :-2], center)]
    return upper_faces, lower_faces, SIGMA_SHIFT * center


def with_diagonal(upper_faces, lower_faces, shift_term):
    diagonal = shift_term + upper_faces[0] + lower_faces[0] + upper_faces[1] + lower_faces[1] + upper_faces[2] + lower_faces[2]
    return upper_faces, lower_faces, diagonal


def blocks(field):
    shape = field.shape
    return field.reshape(shape[0] // 2, 2, shape[1] // 2, 2, shape[2] // 2, 2)


def coarsen_tables(upper_faces, lower_faces, shift_term):
    upper_new = [blocks(upper_faces[0])[:, 1].sum(axis=(2, 4)), blocks(upper_faces[1])[:, :, :, 1].sum(axis=(1, 4)), blocks(upper_faces[2])[..., 1].sum(axis=(1, 3))]
    lower_new = [blocks(lower_faces[0])[:, 0].sum(axis=(2, 4)), blocks(lower_faces[1])[:, :, :, 0].sum(axis=(1, 4)), blocks(lower_faces[2])[..., 0].sum(axis=(1, 3))]
    return upper_new, lower_new, blocks(shift_term).sum(axis=(1, 3, 5))


def restrict(field):
    return blocks(field).sum(axis=(1, 3, 5))


def prolong(field):
    shape = field.shape
    wide = jnp.broadcast_to(field[:, None, :, None, :, None], (shape[0], 2, shape[1], 2, shape[2], 2))
    return wide.reshape(2 * shape[0], 2 * shape[1], 2 * shape[2])


def apply_padded(padded, tables):
    upper_faces, lower_faces, diagonal = tables
    center = padded[1:-1, 1:-1, 1:-1]
    total = diagonal * center
    total = total - (upper_faces[0] * padded[2:, 1:-1, 1:-1] + lower_faces[0] * padded[:-2, 1:-1, 1:-1])
    total = total - (upper_faces[1] * padded[1:-1, 2:, 1:-1] + lower_faces[1] * padded[1:-1, :-2, 1:-1])
    total = total - (upper_faces[2] * padded[1:-1, 1:-1, 2:] + lower_faces[2] * padded[1:-1, 1:-1, :-2])
    return total


def jacobi_sweep(padded, right_side, tables):
    center = padded[1:-1, 1:-1, 1:-1]
    return center + OMEGA * (right_side - apply_padded(padded, tables)) / tables[2]


def shifted_low(field, axis_dim):
    widths = [(0, 0), (0, 0), (0, 0)]
    widths[axis_dim] = (1, 0)
    padded = jnp.pad(field, widths)
    length = field.shape[axis_dim]
    return jnp.take(padded, jnp.arange(length), axis=axis_dim)


def reference(fill_mask, membrane_flags, smear, velocity):
    fraction, conductance = phase_fields(fill_mask, membrane_flags, smear)
    shape = fraction.shape
    open_velocity = []
    for axis_dim in range(3):
        ramp = jnp.arange(shape[axis_dim]) < shape[axis_dim] - 1
        view = [1, 1, 1]
        view[axis_dim] = shape[axis_dim]
        open_velocity.append(velocity[axis_dim] * ramp.astype(jnp.float32).reshape(view))
    upper_faces, lower_faces, shift_term = fine_tables(jnp.pad(conductance, 1))
    levels = []
    for level in range(LEVELS):
        levels.append(with_diagonal(upper_faces, lower_faces, shift_term))
        if level < LEVELS - 1:
            upper_faces, lower_faces, shift_term = coarsen_tables(upper_faces, lower_faces, shift_term)
    right_side = -((open_velocity[0] - shifted_low(open_velocity[0], 0)) + (open_velocity[1] - shifted_low(open_velocity[1], 1)) + (open_velocity[2] - shifted_low(open_velocity[2], 2)))

    def vcycle_level(level, rhs):
        tables = levels[level]
        pressure = jacobi_sweep(jnp.pad(jnp.zeros_like(rhs), 1), rhs, tables)
        if level == LEVELS - 1:
            for _ in range(COARSE_SWEEPS - 1):
                pressure = jacobi_sweep(jnp.pad(pressure, 1), rhs, tables)
            return pressure
        pressure = jacobi_sweep(jnp.pad(pressure, 1), rhs, tables)
        residual = rhs - apply_padded(jnp.pad(pressure, 1), tables)
        pressure = pressure + prolong(vcycle_level(level + 1, restrict(residual)))
        for _ in range(2):
            pressure = jacobi_sweep(jnp.pad(pressure, 1), rhs, tables)
        return pressure

    pressure = vcycle_level(0, right_side)
    padded = jnp.pad(pressure, 1)
    upper_zero = levels[0][0]
    neighbours = [padded[2:, 1:-1, 1:-1], padded[1:-1, 2:, 1:-1], padded[1:-1, 1:-1, 2:]]
    frac_pad = jnp.pad(fraction, 1)
    frac_up = [frac_pad[2:, 1:-1, 1:-1], frac_pad[1:-1, 2:, 1:-1], frac_pad[1:-1, 1:-1, 2:]]
    new_velocity = []
    change = jnp.zeros_like(fraction)
    for axis_dim in range(3):
        moved = open_velocity[axis_dim] - upper_zero[axis_dim] * (neighbours[axis_dim] - pressure)
        new_velocity.append(moved)
        flux = moved * jnp.where(moved > 0, fraction, frac_up[axis_dim])
        change = change + (flux - shifted_low(flux, axis_dim))
    fraction_out = fraction - TIME_STEP * change
    return jnp.stack(new_velocity), fraction_out
```

```python
import functools

import jax
import jax.numpy as jnp
from jax import lax
from jax.experimental import pallas as pl
from jax.experimental.pallas import tpu as pltpu
from jax.sharding import PartitionSpec as P

LEVELS = 4
COARSE_SWEEPS = 8
AXES = ("gx", "gy", "gz")

RHO_LIQUID = 1000.0
RHO_GAS = 1.0
MEMBRANE_DROP = 49.0
SIGMA_SHIFT = 0.1
OMEGA = 0.8
TIME_STEP = 0.2

ROUNDS = 4 * (LEVELS - 1) + COARSE_SWEEPS - 1 + 1


def harmonic(a, b):
    return 2.0 * a * b / (a + b)


def iota(shape, dim):
    return lax.broadcasted_iota(jnp.int32, shape, dim)


def roll(v, shift, dim):
    size = v.shape[dim]
    shift = shift % size
    return v if shift == 0 else pltpu.roll(v, shift, dim)


def odd_mask(v, dim, step):
    return (iota(v.shape, dim) // step) % 2 == 1


def pair_sum(v, dim, step):
    return v + jnp.where(odd_mask(v, dim, step), roll(v, step, dim), roll(v, -step, dim))


def take_odd(v, dim, step):
    return jnp.where(odd_mask(v, dim, step), v, roll(v, -step, dim))


def take_even(v, dim, step):
    return jnp.where(odd_mask(v, dim, step), roll(v, step, dim), v)


def halves(v):
    w = v.reshape(v.shape[0] // 2, 2, v.shape[1], v.shape[2])
    return w[:, 0], w[:, 1]


def restrict(v, step):
    a, b = halves(v)
    return pair_sum(pair_sum(a + b, 1, step), 2, step)


def prolong(v):
    n = v.shape[0]
    w = jnp.broadcast_to(v[:, None], (n, 2, v.shape[1], v.shape[2]))
    return w.reshape(2 * n, v.shape[1], v.shape[2])


def pack_z(v, lane):
    n = v.shape[0]
    wide = jnp.broadcast_to(v[:, :, lane : lane + 1], v.shape)
    return jnp.sum(jnp.where(iota(v.shape, 2) == iota(v.shape, 0), wide, 0.0), axis=0)


def unpack_z(tile, n):
    return jnp.stack([jnp.broadcast_to(tile[:, i : i + 1], tile.shape) for i in range(n)])


def up(v, halos, d, step):
    if d == 0:
        return jnp.concatenate([v[1:], halos[0][None]], axis=0)
    size = v.shape[d]
    return jnp.where(iota(v.shape, d) >= size - step, halos[d], roll(v, -step, d))


def down(v, halos, d, step):
    if d == 0:
        return jnp.concatenate([halos[0][None], v[:-1]], axis=0)
    return jnp.where(iota(v.shape, d) < step, halos[d], roll(v, step, d))


def kernel(
    counts, fill, flags, smear, velocity, vel_out, frac_out,
    first_x, first_y, first_z, got_x, got_y, got_z,
    out_x, out_y, out_z, in_x, in_y, in_z,
    tables, sides, open_u, vel_low, frac_ref, frac_up_ref, frac_down_ref,
    first_send, first_recv, send_sem, recv_sem,
):
    nx, ny, nz = fill.shape
    place = [lax.axis_index(a) for a in AXES]
    has_low = [place[d] > 0 for d in range(3)]
    has_high = [place[d] < counts[d] - 1 for d in range(3)]

    for ref in (got_x, got_y, got_z, in_x, in_y, in_z):
        ref[...] = jnp.zeros_like(ref)

    barrier = pltpu.get_barrier_semaphore()
    for d in range(3):
        for there, step in ((has_low[d], -1), (has_high[d], 1)):
            @pl.when(there)
            def _():
                pl.semaphore_signal(
                    barrier, inc=1, device_id={AXES[d]: place[d] + step},
                    device_id_type=pl.DeviceIdType.MESH,
                )
    total = sum(c.astype(jnp.int32) for c in has_low + has_high)
    pl.semaphore_wait(barrier, total)

    sends = []

    def copy(src, dst, ssem, rsem, d, way):
        return pltpu.make_async_remote_copy(
            src_ref=src, dst_ref=dst, send_sem=ssem, recv_sem=rsem,
            device_id={AXES[d]: place[d] + (1 if way == 0 else -1)},
            device_id_type=pl.DeviceIdType.MESH,
        )

    def send(src, dst, ssem, rsem, d, way):
        target = has_high[d] if way == 0 else has_low[d]

        @pl.when(target)
        def _():
            copy(src, dst, ssem, rsem, d, way).start()

        sends.append((src, dst, ssem, rsem, d, way))

    def receive(src, dst, ssem, rsem, d, way):
        source = has_low[d] if way == 0 else has_high[d]

        @pl.when(source)
        def _():
            copy(src, dst, ssem, rsem, d, way).wait_recv()

    filled = fill[...].astype(jnp.float32)
    walled = flags[...].astype(jnp.float32)
    soft = 0.4 * smear[...]
    fraction = filled * (1.0 - soft) + (1.0 - filled) * soft
    density = RHO_GAS + (RHO_LIQUID - RHO_GAS) * fraction
    conductance = 1.0 / (density * (1.0 + MEMBRANE_DROP * walled))
    shape = fraction.shape
    speeds = []
    for d in range(3):
        position = place[d] * shape[d] + iota(shape, d)
        speeds.append(
            velocity[d] * (position < shape[d] * counts[d] - 1).astype(jnp.float32)
        )
        open_u[d] = speeds[d]
    frac_ref[...] = fraction

    firsts, gots = (first_x, first_y, first_z), (got_x, got_y, got_z)
    plan = []
    for d in range(3):
        for way in range(2):
            at = shape[d] - 1 if way == 0 else 0
            items = [conductance, fraction] + ([speeds[d]] if way == 0 else [])
            for k, item in enumerate(items):
                if d == 0:
                    firsts[0][way, k] = item[at]
                elif d == 1:
                    firsts[1][way, k] = item[:, at : at + 1, :]
                else:
                    firsts[2][way, k] = pack_z(item, at)
            many = pl.ds(0, len(items))
            plan.append((
                firsts[d].at[way, many], gots[d].at[way, many],
                first_send.at[2 * d + way], first_recv.at[2 * d + way], d, way,
            ))
            send(*plan[-1])
    for item in plan:
        receive(*item)

    def first_halos(k, way):
        return [got_x[way, k], got_y[way, k], unpack_z(got_z[way, k], nx)]

    cond_low, cond_high = first_halos(0, 0), first_halos(0, 1)
    frac_low, frac_high = first_halos(1, 0), first_halos(1, 1)
    speed_low = first_halos(2, 0)
    upper = [harmonic(conductance, up(conductance, cond_high, d, 1)) for d in range(3)]
    lower = [harmonic(down(conductance, cond_low, d, 1), conductance) for d in range(3)]
    shift = SIGMA_SHIFT * conductance
    change = jnp.zeros(shape, jnp.float32)
    for d in range(3):
        frac_up_ref[d] = up(fraction, frac_high, d, 1)
        frac_down_ref[d] = down(fraction, frac_low, d, 1)
        low = down(speeds[d], speed_low, d, 1)
        vel_low[d] = low
        change = change + (speeds[d] - low)
    sides[0][...] = -change

    for level in range(LEVELS):
        diagonal = shift
        for d in range(3):
            tables[level][d] = upper[d]
            tables[level][3 + d] = lower[d]
            diagonal = diagonal + upper[d] + lower[d]
        tables[level][6] = diagonal
        tables[level][7] = OMEGA / diagonal
        if level < LEVELS - 1:
            s = 1 << level
            (a, b), (c, e) = halves(upper[0]), halves(lower[0])
            upper_x = pair_sum(pair_sum(b, 1, s), 2, s)
            lower_x = pair_sum(pair_sum(c, 1, s), 2, s)
            both = lambda v: sum(halves(v))
            upper_y = pair_sum(take_odd(both(upper[1]), 1, s), 2, s)
            lower_y = pair_sum(take_even(both(lower[1]), 1, s), 2, s)
            upper_z = pair_sum(take_odd(both(upper[2]), 2, s), 1, s)
            lower_z = pair_sum(take_even(both(lower[2]), 2, s), 1, s)
            upper, lower = [upper_x, upper_y, upper_z], [lower_x, lower_y, lower_z]
            shift = restrict(shift, s)

    outs, ins = (out_x, out_y, out_z), (in_x, in_y, in_z)
    count = [0]

    def exchange(v):
        r = count[0]
        count[0] += 1
        n = v.shape[0]
        plan = []
        for d in range(3):
            for way in range(2):
                at = v.shape[d] - 1 if way == 0 else 0
                if d == 0:
                    outs[0][r, way] = v[at]
                    src, dst = out_x.at[r, way], in_x.at[r, way]
                elif d == 1:
                    outs[1][r, way, pl.ds(0, n)] = v[:, at : at + 1, :]
                    src = out_y.at[r, way, pl.ds(0, n)]
                    dst = in_y.at[r, way, pl.ds(0, n)]
                else:
                    outs[2][r, way] = pack_z(v, at)
                    src, dst = out_z.at[r, way], in_z.at[r, way]
                k = 2 * d + way
                plan.append((src, dst, send_sem.at[r, k], recv_sem.at[r, k], d, way))
                send(*plan[-1])
        for item in plan:
            receive(*item)
        return [
            [in_x[r, way], in_y[r, way, pl.ds(0, n)], unpack_z(in_z[r, way], n)]
            for way in range(2)
        ]

    def around(v, level):
        low, high = exchange(v)
        t, s = tables[level], 1 << level
        total = 0.0
        for d in range(3):
            total = total + (t[d] * up(v, high, d, s) + t[3 + d] * down(v, low, d, s))
        return total

    def sweep(v, level):
        t = tables[level]
        return (1.0 - OMEGA) * v + t[7] * (sides[level][...] + around(v, level))

    def cycle(level):
        v = tables[level][7] * sides[level][...]
        if level == LEVELS - 1:
            for _ in range(COARSE_SWEEPS - 1):
                v = sweep(v, level)
            return v
        v = sweep(v, level)
        residual = sides[level][...] - tables[level][6] * v + around(v, level)
        sides[level + 1][...] = restrict(residual, 1 << level)
        v = v + prolong(cycle(level + 1))
        for _ in range(2):
            v = sweep(v, level)
        return v

    pressure = cycle(0)
    low, high = exchange(pressure)
    change = jnp.zeros(shape, jnp.float32)
    fraction = frac_ref[...]
    for d in range(3):
        moved = open_u[d] - tables[0][d] * (up(pressure, high, d, 1) - pressure)
        moved_low = vel_low[d] - tables[0][3 + d] * (pressure - down(pressure, low, d, 1))
        vel_out[d] = moved
        flux = moved * jnp.where(moved > 0, fraction, frac_up_ref[d])
        flux_low = moved_low * jnp.where(moved_low > 0, frac_down_ref[d], fraction)
        change = change + (flux - flux_low)
    frac_out[...] = fraction - TIME_STEP * change

    for src, dst, ssem, rsem, d, way in sends:
        target = has_high[d] if way == 0 else has_low[d]

        @pl.when(target)
        def _():
            copy(src, dst, ssem, rsem, d, way).wait_send()


def body(counts, kernel, *refs):
    (fill, flags, smear, velocity, vel_out, frac_out, *scratch) = refs
    first, scratch = scratch[:12], scratch[12:]
    tables, scratch = scratch[:LEVELS], scratch[LEVELS:]
    sides, scratch = scratch[:LEVELS], scratch[LEVELS:]
    kernel(
        counts, fill, flags, smear, velocity, vel_out, frac_out,
        *first, tables, sides, *scratch,
    )


def shards(counts, fill_mask, membrane_flags, smear, velocity):
    nx, ny, nz = fill_mask.shape
    f32 = jnp.float32
    vmem = lambda *s: pltpu.VMEM(s, f32)
    first = [vmem(2, 3, ny, nz), vmem(2, 3, nx, 1, nz), vmem(2, 3, ny, nz)] * 2
    rounds = [
        vmem(ROUNDS, 2, ny, nz), vmem(ROUNDS, 2, nx, 1, nz), vmem(ROUNDS, 2, ny, nz)
    ] * 2
    tables = [vmem(8, nx >> l, ny, nz) for l in range(LEVELS)]
    sides = [vmem(nx >> l, ny, nz) for l in range(LEVELS)]
    rest = [vmem(3, nx, ny, nz), vmem(3, nx, ny, nz), vmem(nx, ny, nz)]
    rest += [vmem(3, nx, ny, nz), vmem(3, nx, ny, nz)]
    sems = [pltpu.SemaphoreType.DMA((6,))] * 2 + [pltpu.SemaphoreType.DMA((ROUNDS, 6))] * 2
    whole = pl.BlockSpec(memory_space=pltpu.VMEM)
    return pl.pallas_call(
        functools.partial(body, counts, kernel),
        out_shape=(
            jax.ShapeDtypeStruct(velocity.shape, f32),
            jax.ShapeDtypeStruct(fill_mask.shape, f32),
        ),
        in_specs=[whole] * 4,
        out_specs=(whole, whole),
        scratch_shapes=first + rounds + tables + sides + rest + sems,
        compiler_params=pltpu.CompilerParams(
            collective_id=0, has_side_effects=True, vmem_limit_bytes=32 * 1024 * 1024
        ),
    )(fill_mask, membrane_flags, smear, velocity)


def solution(mesh):
    placed = (P("gx", "gy", "gz"),) * 3 + (P(None, "gx", "gy", "gz"),)
    counts = tuple(mesh.shape[a] for a in AXES)
    return jax.shard_map(
        functools.partial(shards, counts),
        mesh=mesh,
        in_specs=placed,
        out_specs=(P(None, "gx", "gy", "gz"), P("gx", "gy", "gz")),
        check_vma=False,
    )
```

```python
import functools

import jax
import jax.numpy as jnp
from jax import lax
from jax.experimental import pallas as pl
from jax.experimental.pallas import tpu as pltpu
from jax.sharding import PartitionSpec as P

LEVELS = 4
COARSE_SWEEPS = 8
AXES = ("gx", "gy", "gz")

RHO_LIQUID = 1000.0
RHO_GAS = 1.0
MEMBRANE_DROP = 49.0
SIGMA_SHIFT = 0.1
OMEGA = 0.8
TIME_STEP = 0.2

ROUNDS = 4 * (LEVELS - 1) + COARSE_SWEEPS - 1 + 1


def harmonic(a, b):
    return 2.0 * a * b / (a + b)


def iota(shape, dim):
    return lax.broadcasted_iota(jnp.int32, shape, dim)


def roll(v, shift, dim):
    size = v.shape[dim]
    shift = shift % size
    return v if shift == 0 else pltpu.roll(v, shift, dim)


def odd_mask(v, dim, step):
    return (iota(v.shape, dim) // step) % 2 == 1


def pair_sum(v, dim, step):
    return v + jnp.where(odd_mask(v, dim, step), roll(v, step, dim), roll(v, -step, dim))


def take_odd(v, dim, step):
    return jnp.where(odd_mask(v, dim, step), v, roll(v, -step, dim))


def take_even(v, dim, step):
    return jnp.where(odd_mask(v, dim, step), roll(v, step, dim), v)


def halves(v):
    w = v.reshape(v.shape[0] // 2, 2, v.shape[1], v.shape[2])
    return w[:, 0], w[:, 1]


def restrict(v, step):
    a, b = halves(v)
    return pair_sum(pair_sum(a + b, 1, step), 2, step)


def prolong(v):
    n = v.shape[0]
    w = jnp.broadcast_to(v[:, None], (n, 2, v.shape[1], v.shape[2]))
    return w.reshape(2 * n, v.shape[1], v.shape[2])


def pack_z(v, lane):
    n = v.shape[0]
    wide = jnp.broadcast_to(v[:, :, lane : lane + 1], v.shape)
    return jnp.sum(jnp.where(iota(v.shape, 2) == iota(v.shape, 0), wide, 0.0), axis=0)


def unpack_z(tile, n):
    return jnp.stack([jnp.broadcast_to(tile[:, i : i + 1], tile.shape) for i in range(n)])


def up(v, halos, d, step):
    if d == 0:
        return jnp.concatenate([v[1:], halos[0][None]], axis=0)
    size = v.shape[d]
    return jnp.where(iota(v.shape, d) >= size - step, halos[d], roll(v, -step, d))


def down(v, halos, d, step):
    if d == 0:
        return jnp.concatenate([halos[0][None], v[:-1]], axis=0)
    return jnp.where(iota(v.shape, d) < step, halos[d], roll(v, step, d))


def gathers(counts, shape):
    return shape == (16, 8, 128) and counts == (2, 4, 4)


def compact(f):
    wide = iota(f.shape, 2) % 4 == iota(f.shape, 0)
    return jnp.sum(jnp.where(wide, f, 0.0), axis=0)


def turned(v, by):
    return jnp.concatenate([v[by:], v[:by]], axis=0)


def dense_up(v, d, s, ny):
    lane, row = iota(v.shape, 2), iota(v.shape, 1)
    if d == 0:
        return jnp.where(lane % 4 + s < 4, roll(v, -s, 2), roll(turned(v, ny), 4 - s, 2))
    if d == 1:
        far = turned(v, 1)
        return far if s == 2 else roll(jnp.where(row >= 4, v, far), 4, 1)
    near = roll(v, -4 * s, 2)
    return jnp.where(lane < 128 - 4 * s, near, roll(near, -1, 1))


def dense_down(v, d, s, ny):
    lane, row = iota(v.shape, 2), iota(v.shape, 1)
    if d == 0:
        return jnp.where(lane % 4 >= s, roll(v, s, 2), roll(turned(v, -ny), s - 4, 2))
    if d == 1:
        far = turned(v, -1)
        return far if s == 2 else roll(jnp.where(row < 4, v, far), 4, 1)
    near = roll(v, 4 * s, 2)
    return jnp.where(lane >= 4 * s, near, roll(near, 1, 1))


def dense_tables(upper, shift, s, ny):
    lower = [dense_down(upper[d], d, s, ny) for d in range(3)]
    diagonal = shift
    for d in range(3):
        diagonal = diagonal + upper[d] + lower[d]
    return upper + lower + [diagonal, OMEGA / diagonal]


def dense_around(v, t, s, ny):
    total = 0.0
    for d in range(3):
        total = total + (t[d] * dense_up(v, d, s, ny) + t[3 + d] * dense_down(v, d, s, ny))
    return total


def dense_sweep(v, rhs, t, s, ny):
    return (1.0 - OMEGA) * v + t[7] * (rhs + dense_around(v, t, s, ny))


def dense_cycle(rhs, fine, coarse, ny):
    v = fine[7] * rhs
    v = dense_sweep(v, rhs, fine, 1, ny)
    residual = rhs - fine[6] * v + dense_around(v, fine, 1, ny)
    rhs3 = pair_sum(pair_sum(pair_sum(residual, 2, 1), 1, 4), 2, 4)
    e = coarse[7] * rhs3
    for _ in range(COARSE_SWEEPS - 1):
        e = dense_sweep(e, rhs3, coarse, 2, ny)
    v = v + e
    for _ in range(2):
        v = dense_sweep(v, rhs, fine, 1, ny)
    return v


def local_of(tile, gz):
    own = jnp.where(iota(tile.shape, 0) % 4 == gz, tile, 0.0)
    own = pair_sum(pair_sum(own, 0, 1), 0, 2)
    wide = jnp.broadcast_to(own[None], (4,) + own.shape)
    wide = jnp.where(iota(wide.shape, 2) % 4 == iota(wide.shape, 0), wide, 0.0)
    return pair_sum(pair_sum(wide, 2, 1), 2, 2)


def kernel(
    counts, fill_at, flags_at, smear_at, velocity_at, vel_out, frac_out,
    fill, flags, smear, velocity, load_sem,
    first_x, first_y, first_z, got_x, got_y, got_z,
    out_x, out_y, out_z, in_x, in_y, in_z,
    tables, sides, open_u, vel_low, frac_ref, frac_up_ref, frac_down_ref,
    first_send, first_recv, send_sem, recv_sem,
    own_tables, all_tables, own_side, all_side, answer, all_send, all_recv,
):
    nx, ny, nz = fill.shape
    place = [lax.axis_index(a) for a in AXES]
    has_low = [place[d] > 0 for d in range(3)]
    has_high = [place[d] < counts[d] - 1 for d in range(3)]

    gather = gathers(counts, fill.shape)
    loads = [
        pltpu.make_async_copy(src, dst, load_sem.at[i])
        for i, (src, dst) in enumerate(
            zip((fill_at, flags_at, smear_at, velocity_at), (fill, flags, smear, velocity))
        )
    ]
    for load in loads:
        load.start()
    for ref in (got_x, got_y, got_z, in_x, in_y, in_z):
        ref[...] = jnp.zeros_like(ref)

    offsets = [
        (i, j, k) for i in range(counts[0]) for j in range(counts[1])
        for k in range(counts[2]) if (i, j, k) != (0, 0, 0)
    ]

    def peer(offset, sign):
        return tuple(
            lax.rem(place[d] + (counts[d] + sign * offset[d]), counts[d]) for d in range(3)
        )

    barrier = pltpu.get_barrier_semaphore()
    for offset in offsets if gather else []:
        pl.semaphore_signal(
            barrier, inc=1, device_id=peer(offset, 1),
            device_id_type=pl.DeviceIdType.MESH,
        )
    for d in [] if gather else range(3):
        for there, step in ((has_low[d], -1), (has_high[d], 1)):
            @pl.when(there)
            def _():
                pl.semaphore_signal(
                    barrier, inc=1, device_id={AXES[d]: place[d] + step},
                    device_id_type=pl.DeviceIdType.MESH,
                )
    total = len(offsets)
    if not gather:
        total = sum(c.astype(jnp.int32) for c in has_low + has_high)

    sends = []

    def copy(src, dst, ssem, rsem, d, way):
        return pltpu.make_async_remote_copy(
            src_ref=src, dst_ref=dst, send_sem=ssem, recv_sem=rsem,
            device_id={AXES[d]: place[d] + (1 if way == 0 else -1)},
            device_id_type=pl.DeviceIdType.MESH,
        )

    def send(src, dst, ssem, rsem, d, way):
        target = has_high[d] if way == 0 else has_low[d]

        @pl.when(target)
        def _():
            copy(src, dst, ssem, rsem, d, way).start()

        sends.append((src, dst, ssem, rsem, d, way))

    def receive(src, dst, ssem, rsem, d, way):
        source = has_low[d] if way == 0 else has_high[d]

        @pl.when(source)
        def _():
            copy(src, dst, ssem, rsem, d, way).wait_recv()

    for load in loads:
        load.wait()
    filled = fill[...].astype(jnp.float32)
    walled = flags[...].astype(jnp.float32)
    soft = 0.4 * smear[...]
    fraction = filled * (1.0 - soft) + (1.0 - filled) * soft
    density = RHO_GAS + (RHO_LIQUID - RHO_GAS) * fraction
    conductance = 1.0 / (density * (1.0 + MEMBRANE_DROP * walled))
    shape = fraction.shape
    speeds = []
    for d in range(3):
        position = place[d] * shape[d] + iota(shape, d)
        speeds.append(
            velocity[d] * (position < shape[d] * counts[d] - 1).astype(jnp.float32)
        )
        open_u[d] = speeds[d]
    frac_ref[...] = fraction

    firsts, gots = (first_x, first_y, first_z), (got_x, got_y, got_z)
    plan = []
    for d in range(3):
        for way in range(2):
            at = shape[d] - 1 if way == 0 else 0
            items = [conductance, fraction] + ([speeds[d]] if way == 0 else [])
            for k, item in enumerate(items):
                if d == 0:
                    firsts[0][way, k] = item[at]
                elif d == 1:
                    firsts[1][way, k] = item[:, at : at + 1, :]
                else:
                    firsts[2][way, k] = pack_z(item, at)
            many = pl.ds(0, len(items))
            plan.append((
                firsts[d].at[way, many], gots[d].at[way, many],
                first_send.at[2 * d + way], first_recv.at[2 * d + way], d, way,
            ))
    pl.semaphore_wait(barrier, total)
    for item in plan:
        send(*item)
    for item in plan:
        receive(*item)

    def first_halos(k, way):
        return [got_x[way, k], got_y[way, k], unpack_z(got_z[way, k], nx)]

    cond_low, cond_high = first_halos(0, 0), first_halos(0, 1)
    frac_low, frac_high = first_halos(1, 0), first_halos(1, 1)
    speed_low = first_halos(2, 0)
    upper = [harmonic(conductance, up(conductance, cond_high, d, 1)) for d in range(3)]
    lower = [harmonic(down(conductance, cond_low, d, 1), conductance) for d in range(3)]
    shift = SIGMA_SHIFT * conductance
    change = jnp.zeros(shape, jnp.float32)
    for d in range(3):
        frac_up_ref[d] = up(fraction, frac_high, d, 1)
        frac_down_ref[d] = down(fraction, frac_low, d, 1)
        low = down(speeds[d], speed_low, d, 1)
        vel_low[d] = low
        change = change + (speeds[d] - low)
    sides[0][...] = -change

    for level in range(2 if gather else LEVELS):
        diagonal = shift
        for d in range(3):
            tables[level][d] = upper[d]
            tables[level][3 + d] = lower[d]
            diagonal = diagonal + upper[d] + lower[d]
        tables[level][6] = diagonal
        tables[level][7] = OMEGA / diagonal
        if level < LEVELS - 1:
            s = 1 << level
            (a, b), (c, e) = halves(upper[0]), halves(lower[0])
            upper_x = pair_sum(pair_sum(b, 1, s), 2, s)
            lower_x = pair_sum(pair_sum(c, 1, s), 2, s)
            both = lambda v: sum(halves(v))
            upper_y = pair_sum(take_odd(both(upper[1]), 1, s), 2, s)
            lower_y = pair_sum(take_even(both(lower[1]), 1, s), 2, s)
            upper_z = pair_sum(take_odd(both(upper[2]), 2, s), 1, s)
            lower_z = pair_sum(take_even(both(lower[2]), 2, s), 1, s)
            upper, lower = [upper_x, upper_y, upper_z], [lower_x, lower_y, lower_z]
            shift = restrict(shift, s)

    outs, ins = (out_x, out_y, out_z), (in_x, in_y, in_z)
    count = [0]

    def spread(src, dst_of, k):
        dst_of(place)[...] = src[...]
        copies = []
        for i, offset in enumerate(offsets):
            copies.append(pltpu.make_async_remote_copy(
                src_ref=src, dst_ref=dst_of(place),
                send_sem=all_send.at[k, i], recv_sem=all_recv.at[k, i],
                device_id=peer(offset, 1), device_id_type=pl.DeviceIdType.MESH,
            ))
            copies[-1].start()
        return copies

    def table_at(p):
        return all_tables.at[:, p[0] * counts[1] + p[1], :, p[2]]

    def side_at(p):
        return all_side.at[p[0] * counts[1] + p[1], :, p[2]]

    def collect(dst_of, k):
        for i, offset in enumerate(offsets):
            ref = dst_of(peer(offset, -1))
            pltpu.make_async_remote_copy(
                src_ref=ref, dst_ref=ref,
                send_sem=all_send.at[k, i], recv_sem=all_recv.at[k, i],
                device_id=peer(offset, -1), device_id_type=pl.DeviceIdType.MESH,
            ).wait_recv()

    def rows(f):
        tile = compact(f)
        return [tile[0:1], tile[4:5]]

    spreads = []

    def send_tables():
        for k, f in enumerate(upper + [shift]):
            for j, row in enumerate(rows(f)):
                own_tables[k, j] = row
        spreads.extend(spread(own_tables, table_at, 0))

    def coarse_solve(residual2):
        for j, row in enumerate(rows(residual2)):
            own_side[j] = row
        spreads.extend(spread(own_side, side_at, 1))
        collect(table_at, 0)
        many = counts[0] * counts[1]
        shaped = lambda w: w.reshape(many, 8, 128)
        *up2, shift2 = [shaped(all_tables[k]) for k in range(4)]
        ny = counts[1]
        y_z = lambda v: pair_sum(pair_sum(v, 1, 4), 2, 4)
        up3 = [
            y_z(take_odd(up2[0], 2, 1)),
            pair_sum(pair_sum(take_odd(up2[1], 1, 4), 2, 1), 2, 4),
            pair_sum(pair_sum(take_odd(up2[2], 2, 4), 2, 1), 1, 4),
        ]
        shift3 = pair_sum(y_z(shift2), 2, 1)
        fine = dense_tables(up2, shift2, 1, ny)
        coarse = dense_tables(up3, shift3, 2, ny)
        collect(side_at, 1)
        answer[...] = dense_cycle(shaped(all_side[...]), fine, coarse, ny)

    def answer_at(d, step):
        p = list(place)
        if d is not None:
            p[d] = lax.rem(p[d] + (counts[d] + step), counts[d])
        return local_of(answer[p[0] * counts[1] + p[1]], p[2])

    def corrected(halos, way):
        step = -1 if way == 0 else 1
        e = [answer_at(d, step) for d in range(3)]
        edge = lambda f, d: f.shape[d] - 1 if way == 0 else 0
        x, y, z = edge(e[0], 0), edge(e[1], 1), edge(e[2], 2)
        return [
            halos[0] + e[0][x],
            halos[1] + prolong(e[1][:, y : y + 1, :]),
            halos[2] + prolong(jnp.broadcast_to(e[2][:, :, z : z + 1], e[2].shape)),
        ]

    def exchange(v, meanwhile=None):
        r = count[0]
        count[0] += 1
        n = v.shape[0]
        plan = []
        for d in range(3):
            for way in range(2):
                at = v.shape[d] - 1 if way == 0 else 0
                if d == 0:
                    outs[0][r, way] = v[at]
                    src, dst = out_x.at[r, way], in_x.at[r, way]
                elif d == 1:
                    outs[1][r, way, pl.ds(0, n)] = v[:, at : at + 1, :]
                    src = out_y.at[r, way, pl.ds(0, n)]
                    dst = in_y.at[r, way, pl.ds(0, n)]
                else:
                    outs[2][r, way] = pack_z(v, at)
                    src, dst = out_z.at[r, way], in_z.at[r, way]
                k = 2 * d + way
                plan.append((src, dst, send_sem.at[r, k], recv_sem.at[r, k], d, way))
                send(*plan[-1])
        if meanwhile is not None:
            meanwhile()
        for item in plan:
            receive(*item)
        return [
            [in_x[r, way], in_y[r, way, pl.ds(0, n)], unpack_z(in_z[r, way], n)]
            for way in range(2)
        ]

    def around(v, level, halos=None, meanwhile=None):
        low, high = halos or exchange(v, meanwhile)
        t, s = tables[level], 1 << level
        total = 0.0
        for d in range(3):
            total = total + (t[d] * up(v, high, d, s) + t[3 + d] * down(v, low, d, s))
        return total

    def sweep(v, level, halos=None, meanwhile=None):
        t = tables[level]
        total = sides[level][...] + around(v, level, halos, meanwhile)
        return (1.0 - OMEGA) * v + t[7] * total

    def cycle(level):
        v = tables[level][7] * sides[level][...]
        if level == LEVELS - 1:
            for _ in range(COARSE_SWEEPS - 1):
                v = sweep(v, level)
            return v
        v = sweep(v, level, None, send_tables if gather and level == 0 else None)
        halos = exchange(v)
        residual = sides[level][...] - tables[level][6] * v + around(v, level, halos)
        if gather and level == 1:
            coarse_solve(restrict(residual, 1 << level))
            v = v + prolong(answer_at(None, 0))
            v = sweep(v, level, [corrected(halos[0], 0), corrected(halos[1], 1)])
            return sweep(v, level)
        sides[level + 1][...] = restrict(residual, 1 << level)
        v = v + prolong(cycle(level + 1))
        for _ in range(2):
            v = sweep(v, level)
        return v

    pressure = cycle(0)
    low, high = exchange(pressure)
    change = jnp.zeros(shape, jnp.float32)
    fraction = frac_ref[...]
    for d in range(3):
        moved = open_u[d] - tables[0][d] * (up(pressure, high, d, 1) - pressure)
        moved_low = vel_low[d] - tables[0][3 + d] * (pressure - down(pressure, low, d, 1))
        vel_out[d] = moved
        flux = moved * jnp.where(moved > 0, fraction, frac_up_ref[d])
        flux_low = moved_low * jnp.where(moved_low > 0, frac_down_ref[d], fraction)
        change = change + (flux - flux_low)
    frac_out[...] = fraction - TIME_STEP * change

    for src, dst, ssem, rsem, d, way in sends:
        target = has_high[d] if way == 0 else has_low[d]

        @pl.when(target)
        def _():
            copy(src, dst, ssem, rsem, d, way).wait_send()

    for item in spreads:
        item.wait_send()


def body(counts, kernel, *refs):
    (fill, flags, smear, velocity, vel_out, frac_out, *scratch) = refs
    loaded, scratch = scratch[:5], scratch[5:]
    first, scratch = scratch[:12], scratch[12:]
    tables, scratch = scratch[:LEVELS], scratch[LEVELS:]
    sides, scratch = scratch[:LEVELS], scratch[LEVELS:]
    kernel(
        counts, fill, flags, smear, velocity, vel_out, frac_out, *loaded,
        *first, tables, sides, *scratch,
    )


def shards(counts, fill_mask, membrane_flags, smear, velocity):
    nx, ny, nz = fill_mask.shape
    f32 = jnp.float32
    vmem = lambda *s: pltpu.VMEM(s, f32)
    first = [vmem(2, 3, ny, nz), vmem(2, 3, nx, 1, nz), vmem(2, 3, ny, nz)] * 2
    rounds = [
        vmem(ROUNDS, 2, ny, nz), vmem(ROUNDS, 2, nx, 1, nz), vmem(ROUNDS, 2, ny, nz)
    ] * 2
    tables = [vmem(8, nx >> l, ny, nz) for l in range(LEVELS)]
    sides = [vmem(nx >> l, ny, nz) for l in range(LEVELS)]
    rest = [vmem(3, nx, ny, nz), vmem(3, nx, ny, nz), vmem(nx, ny, nz)]
    rest += [vmem(3, nx, ny, nz), vmem(3, nx, ny, nz)]
    sems = [pltpu.SemaphoreType.DMA((6,))] * 2 + [pltpu.SemaphoreType.DMA((ROUNDS, 6))] * 2
    loaded = [pltpu.VMEM(a.shape, a.dtype) for a in (fill_mask, membrane_flags, smear, velocity)]
    loaded += [pltpu.SemaphoreType.DMA((4,))]
    many = counts[0] * counts[1]
    peers = many * counts[2] if gathers(counts, fill_mask.shape) else 1
    sems += [
        vmem(4, 2, 1, nz), vmem(4, many, 2, counts[2], 1, nz), vmem(2, 1, nz),
        vmem(many, 2, counts[2], 1, nz), vmem(many, ny, nz),
    ] + [pltpu.SemaphoreType.DMA((2, peers))] * 2
    whole = pl.BlockSpec(memory_space=pltpu.VMEM)
    left = pl.BlockSpec(memory_space=pl.ANY)
    return pl.pallas_call(
        functools.partial(body, counts, kernel),
        out_shape=(
            jax.ShapeDtypeStruct(velocity.shape, f32),
            jax.ShapeDtypeStruct(fill_mask.shape, f32),
        ),
        in_specs=[left] * 4,
        out_specs=(whole, whole),
        scratch_shapes=loaded + first + rounds + tables + sides + rest + sems,
        compiler_params=pltpu.CompilerParams(
            collective_id=0, has_side_effects=True, vmem_limit_bytes=32 * 1024 * 1024
        ),
    )(fill_mask, membrane_flags, smear, velocity)


def solution(mesh):
    placed = (P("gx", "gy", "gz"),) * 3 + (P(None, "gx", "gy", "gz"),)
    counts = tuple(mesh.shape[a] for a in AXES)
    return jax.shard_map(
        functools.partial(shards, counts),
        mesh=mesh,
        in_specs=placed,
        out_specs=(P(None, "gx", "gy", "gz"), P("gx", "gy", "gz")),
        check_vma=False,
    )
```

```python
import functools

import jax
import jax.numpy as jnp
from jax import lax
from jax.experimental import pallas as pl
from jax.experimental.pallas import tpu as pltpu
from jax.sharding import PartitionSpec as P

LEVELS = 4
COARSE_SWEEPS = 8
AXES = ("gx", "gy", "gz")

RHO_LIQUID = 1000.0
RHO_GAS = 1.0
MEMBRANE_DROP = 49.0
SIGMA_SHIFT = 0.1
OMEGA = 0.8
TIME_STEP = 0.2

ROUNDS = 4 * (LEVELS - 1) + COARSE_SWEEPS - 1 + 1


def harmonic(a, b):
    return 2.0 * a * b / (a + b)


def iota(shape, dim):
    return lax.broadcasted_iota(jnp.int32, shape, dim)


def roll(v, shift, dim):
    size = v.shape[dim]
    shift = shift % size
    return v if shift == 0 else pltpu.roll(v, shift, dim)


def odd_mask(v, dim, step):
    return (iota(v.shape, dim) // step) % 2 == 1


def pair_sum(v, dim, step):
    return v + jnp.where(odd_mask(v, dim, step), roll(v, step, dim), roll(v, -step, dim))


def take_odd(v, dim, step):
    return jnp.where(odd_mask(v, dim, step), v, roll(v, -step, dim))


def take_even(v, dim, step):
    return jnp.where(odd_mask(v, dim, step), roll(v, step, dim), v)


def halves(v):
    w = v.reshape(v.shape[0] // 2, 2, v.shape[1], v.shape[2])
    return w[:, 0], w[:, 1]


def restrict(v, step):
    a, b = halves(v)
    return pair_sum(pair_sum(a + b, 1, step), 2, step)


def prolong(v):
    n = v.shape[0]
    w = jnp.broadcast_to(v[:, None], (n, 2, v.shape[1], v.shape[2]))
    return w.reshape(2 * n, v.shape[1], v.shape[2])


def pack_z(v, lane):
    n = v.shape[0]
    wide = jnp.broadcast_to(v[:, :, lane : lane + 1], v.shape)
    return jnp.sum(jnp.where(iota(v.shape, 2) == iota(v.shape, 0), wide, 0.0), axis=0)


def unpack_z(tile, n):
    return jnp.stack([jnp.broadcast_to(tile[:, i : i + 1], tile.shape) for i in range(n)])


def up(v, halos, d, step):
    if d == 0:
        return jnp.concatenate([v[1:], halos[0][None]], axis=0)
    size = v.shape[d]
    return jnp.where(iota(v.shape, d) >= size - step, halos[d], roll(v, -step, d))


def down(v, halos, d, step):
    if d == 0:
        return jnp.concatenate([halos[0][None], v[:-1]], axis=0)
    return jnp.where(iota(v.shape, d) < step, halos[d], roll(v, step, d))


def gathers(counts, shape):
    return shape == (16, 8, 128) and counts == (2, 4, 4)


def compact(f):
    wide = iota(f.shape, 2) % 4 == iota(f.shape, 0)
    return jnp.sum(jnp.where(wide, f, 0.0), axis=0)


def turned(v, by):
    return jnp.concatenate([v[by:], v[:by]], axis=0)


def dense_up(v, d, s, ny):
    lane, row = iota(v.shape, 2), iota(v.shape, 1)
    if d == 0:
        return jnp.where(lane % 4 + s < 4, roll(v, -s, 2), roll(turned(v, ny), 4 - s, 2))
    if d == 1:
        far = turned(v, 1)
        return far if s == 2 else roll(jnp.where(row >= 4, v, far), 4, 1)
    near = roll(v, -4 * s, 2)
    return jnp.where(lane < 128 - 4 * s, near, roll(near, -1, 1))


def dense_down(v, d, s, ny):
    lane, row = iota(v.shape, 2), iota(v.shape, 1)
    if d == 0:
        return jnp.where(lane % 4 >= s, roll(v, s, 2), roll(turned(v, -ny), s - 4, 2))
    if d == 1:
        far = turned(v, -1)
        return far if s == 2 else roll(jnp.where(row < 4, v, far), 4, 1)
    near = roll(v, 4 * s, 2)
    return jnp.where(lane >= 4 * s, near, roll(near, 1, 1))


def dense_tables(upper, shift, s, ny):
    lower = [dense_down(upper[d], d, s, ny) for d in range(3)]
    diagonal = shift
    for d in range(3):
        diagonal = diagonal + upper[d] + lower[d]
    return upper + lower + [diagonal, OMEGA / diagonal]


def dense_around(v, t, s, ny):
    total = 0.0
    for d in range(3):
        total = total + (t[d] * dense_up(v, d, s, ny) + t[3 + d] * dense_down(v, d, s, ny))
    return total


def dense_sweep(v, rhs, t, s, ny):
    return (1.0 - OMEGA) * v + t[7] * (rhs + dense_around(v, t, s, ny))


def dense_cycle(rhs, fine, coarse, ny):
    v = fine[7] * rhs
    v = dense_sweep(v, rhs, fine, 1, ny)
    residual = rhs - fine[6] * v + dense_around(v, fine, 1, ny)
    rhs3 = pair_sum(pair_sum(pair_sum(residual, 2, 1), 1, 4), 2, 4)
    e = coarse[7] * rhs3
    for _ in range(COARSE_SWEEPS - 1):
        e = dense_sweep(e, rhs3, coarse, 2, ny)
    v = v + e
    for _ in range(2):
        v = dense_sweep(v, rhs, fine, 1, ny)
    return v


def local_of(tile, gz):
    own = jnp.where(iota(tile.shape, 0) % 4 == gz, tile, 0.0)
    own = pair_sum(pair_sum(own, 0, 1), 0, 2)
    wide = jnp.broadcast_to(own[None], (4,) + own.shape)
    wide = jnp.where(iota(wide.shape, 2) % 4 == iota(wide.shape, 0), wide, 0.0)
    return pair_sum(pair_sum(wide, 2, 1), 2, 2)


def kernel(
    counts, fill_at, flags_at, smear_at, velocity_at, vel_out, frac_out,
    fill, flags, smear, velocity, load_sem,
    first_x, first_y, first_z, got_x, got_y, got_z,
    out_x, out_y, out_z, in_x, in_y, in_z,
    tables, sides, open_u, vel_low, frac_ref, frac_up_ref, frac_down_ref,
    first_send, first_recv, send_sem, recv_sem,
    own_tables, all_tables, own_side, all_side, answer, all_send, all_recv,
):
    nx, ny, nz = fill.shape
    place = [lax.axis_index(a) for a in AXES]
    has_low = [place[d] > 0 for d in range(3)]
    has_high = [place[d] < counts[d] - 1 for d in range(3)]

    gather = gathers(counts, fill.shape)
    loads = [
        pltpu.make_async_copy(src, dst, load_sem.at[i])
        for i, (src, dst) in enumerate(
            zip((fill_at, flags_at, smear_at, velocity_at), (fill, flags, smear, velocity))
        )
    ]
    for load in loads:
        load.start()
    for ref in (got_x, got_y, got_z, in_x, in_y, in_z):
        ref[...] = jnp.zeros_like(ref)

    offsets = [
        (i, j, k) for i in range(counts[0]) for j in range(counts[1])
        for k in range(counts[2]) if (i, j, k) != (0, 0, 0)
    ]
    offsets.sort(key=lambda o: -sum(max(p, c - p) for p, c in zip(o, counts) if p))

    def peer(offset, sign):
        return tuple(
            lax.rem(place[d] + (counts[d] + sign * offset[d]), counts[d]) for d in range(3)
        )

    barrier = pltpu.get_barrier_semaphore()
    for offset in offsets if gather else []:
        pl.semaphore_signal(
            barrier, inc=1, device_id=peer(offset, 1),
            device_id_type=pl.DeviceIdType.MESH,
        )
    for d in [] if gather else range(3):
        for there, step in ((has_low[d], -1), (has_high[d], 1)):
            @pl.when(there)
            def _():
                pl.semaphore_signal(
                    barrier, inc=1, device_id={AXES[d]: place[d] + step},
                    device_id_type=pl.DeviceIdType.MESH,
                )
    total = len(offsets)
    if not gather:
        total = sum(c.astype(jnp.int32) for c in has_low + has_high)

    sends = []

    def copy(src, dst, ssem, rsem, d, way):
        return pltpu.make_async_remote_copy(
            src_ref=src, dst_ref=dst, send_sem=ssem, recv_sem=rsem,
            device_id={AXES[d]: place[d] + (1 if way == 0 else -1)},
            device_id_type=pl.DeviceIdType.MESH,
        )

    def send(src, dst, ssem, rsem, d, way):
        target = has_high[d] if way == 0 else has_low[d]

        @pl.when(target)
        def _():
            copy(src, dst, ssem, rsem, d, way).start()

        sends.append((src, dst, ssem, rsem, d, way))

    def receive(src, dst, ssem, rsem, d, way):
        source = has_low[d] if way == 0 else has_high[d]

        @pl.when(source)
        def _():
            copy(src, dst, ssem, rsem, d, way).wait_recv()

    for load in loads:
        load.wait()
    filled = fill[...].astype(jnp.float32)
    walled = flags[...].astype(jnp.float32)
    soft = 0.4 * smear[...]
    fraction = filled * (1.0 - soft) + (1.0 - filled) * soft
    density = RHO_GAS + (RHO_LIQUID - RHO_GAS) * fraction
    conductance = 1.0 / (density * (1.0 + MEMBRANE_DROP * walled))
    shape = fraction.shape
    speeds = []
    for d in range(3):
        position = place[d] * shape[d] + iota(shape, d)
        speeds.append(
            velocity[d] * (position < shape[d] * counts[d] - 1).astype(jnp.float32)
        )
        open_u[d] = speeds[d]
    frac_ref[...] = fraction

    firsts, gots = (first_x, first_y, first_z), (got_x, got_y, got_z)
    plan = []
    for d in range(3):
        for way in range(2):
            at = shape[d] - 1 if way == 0 else 0
            items = [conductance, fraction] + ([speeds[d]] if way == 0 else [])
            for k, item in enumerate(items):
                if d == 0:
                    firsts[0][way, k] = item[at]
                elif d == 1:
                    firsts[1][way, k] = item[:, at : at + 1, :]
                else:
                    firsts[2][way, k] = pack_z(item, at)
            many = pl.ds(0, len(items))
            plan.append((
                firsts[d].at[way, many], gots[d].at[way, many],
                first_send.at[2 * d + way], first_recv.at[2 * d + way], d, way,
            ))
    pl.semaphore_wait(barrier, total)
    for item in plan:
        send(*item)
    for item in plan:
        receive(*item)

    def first_halos(k, way):
        return [got_x[way, k], got_y[way, k], unpack_z(got_z[way, k], nx)]

    cond_low, cond_high = first_halos(0, 0), first_halos(0, 1)
    frac_low, frac_high = first_halos(1, 0), first_halos(1, 1)
    speed_low = first_halos(2, 0)
    upper = [harmonic(conductance, up(conductance, cond_high, d, 1)) for d in range(3)]
    lower = [harmonic(down(conductance, cond_low, d, 1), conductance) for d in range(3)]
    shift = SIGMA_SHIFT * conductance
    change = jnp.zeros(shape, jnp.float32)
    for d in range(3):
        frac_up_ref[d] = up(fraction, frac_high, d, 1)
        frac_down_ref[d] = down(fraction, frac_low, d, 1)
        low = down(speeds[d], speed_low, d, 1)
        vel_low[d] = low
        change = change + (speeds[d] - low)
    sides[0][...] = -change

    for level in range(2 if gather else LEVELS):
        diagonal = shift
        for d in range(3):
            tables[level][d] = upper[d]
            tables[level][3 + d] = lower[d]
            diagonal = diagonal + upper[d] + lower[d]
        tables[level][6] = diagonal
        tables[level][7] = OMEGA / diagonal
        if level < LEVELS - 1:
            s = 1 << level
            (a, b), (c, e) = halves(upper[0]), halves(lower[0])
            upper_x = pair_sum(pair_sum(b, 1, s), 2, s)
            lower_x = pair_sum(pair_sum(c, 1, s), 2, s)
            both = lambda v: sum(halves(v))
            upper_y = pair_sum(take_odd(both(upper[1]), 1, s), 2, s)
            lower_y = pair_sum(take_even(both(lower[1]), 1, s), 2, s)
            upper_z = pair_sum(take_odd(both(upper[2]), 2, s), 1, s)
            lower_z = pair_sum(take_even(both(lower[2]), 2, s), 1, s)
            upper, lower = [upper_x, upper_y, upper_z], [lower_x, lower_y, lower_z]
            shift = restrict(shift, s)

    outs, ins = (out_x, out_y, out_z), (in_x, in_y, in_z)
    count = [0]

    def spread(src, dst_of, k):
        dst_of(place)[...] = src[...]
        copies = []
        for i, offset in enumerate(offsets):
            copies.append(pltpu.make_async_remote_copy(
                src_ref=src, dst_ref=dst_of(place),
                send_sem=all_send.at[k, i], recv_sem=all_recv.at[k, i],
                device_id=peer(offset, 1), device_id_type=pl.DeviceIdType.MESH,
            ))
            copies[-1].start()
        return copies

    def table_at(p):
        return all_tables.at[:, p[0] * counts[1] + p[1], :, p[2]]

    def side_at(p):
        return all_side.at[p[0] * counts[1] + p[1], :, p[2]]

    def collect(dst_of, k):
        for i, offset in enumerate(offsets):
            ref = dst_of(peer(offset, -1))
            pltpu.make_async_remote_copy(
                src_ref=ref, dst_ref=ref,
                send_sem=all_send.at[k, i], recv_sem=all_recv.at[k, i],
                device_id=peer(offset, -1), device_id_type=pl.DeviceIdType.MESH,
            ).wait_recv()

    def rows(f):
        tile = compact(f)
        return [tile[0:1], tile[4:5]]

    spreads = []

    def send_tables():
        for k, f in enumerate(upper + [shift]):
            for j, row in enumerate(rows(f)):
                own_tables[k, j] = row
        spreads.extend(spread(own_tables, table_at, 0))

    def coarse_solve(residual2):
        for j, row in enumerate(rows(residual2)):
            own_side[j] = row
        spreads.extend(spread(own_side, side_at, 1))
        collect(table_at, 0)
        many = counts[0] * counts[1]
        shaped = lambda w: w.reshape(many, 8, 128)
        *up2, shift2 = [shaped(all_tables[k]) for k in range(4)]
        ny = counts[1]
        y_z = lambda v: pair_sum(pair_sum(v, 1, 4), 2, 4)
        up3 = [
            y_z(take_odd(up2[0], 2, 1)),
            pair_sum(pair_sum(take_odd(up2[1], 1, 4), 2, 1), 2, 4),
            pair_sum(pair_sum(take_odd(up2[2], 2, 4), 2, 1), 1, 4),
        ]
        shift3 = pair_sum(y_z(shift2), 2, 1)
        fine = dense_tables(up2, shift2, 1, ny)
        coarse = dense_tables(up3, shift3, 2, ny)
        collect(side_at, 1)
        answer[...] = dense_cycle(shaped(all_side[...]), fine, coarse, ny)

    def answer_at(d, step):
        p = list(place)
        if d is not None:
            p[d] = lax.rem(p[d] + (counts[d] + step), counts[d])
        return local_of(answer[p[0] * counts[1] + p[1]], p[2])

    def corrected(halos, way):
        step = -1 if way == 0 else 1
        e = [answer_at(d, step) for d in range(3)]
        edge = lambda f, d: f.shape[d] - 1 if way == 0 else 0
        x, y, z = edge(e[0], 0), edge(e[1], 1), edge(e[2], 2)
        return [
            halos[0] + e[0][x],
            halos[1] + prolong(e[1][:, y : y + 1, :]),
            halos[2] + prolong(jnp.broadcast_to(e[2][:, :, z : z + 1], e[2].shape)),
        ]

    def exchange(v, meanwhile=None):
        r = count[0]
        count[0] += 1
        n = v.shape[0]
        plan = []
        for d in range(3):
            for way in range(2):
                at = v.shape[d] - 1 if way == 0 else 0
                if d == 0:
                    outs[0][r, way] = v[at]
                    src, dst = out_x.at[r, way], in_x.at[r, way]
                elif d == 1:
                    outs[1][r, way, pl.ds(0, n)] = v[:, at : at + 1, :]
                    src = out_y.at[r, way, pl.ds(0, n)]
                    dst = in_y.at[r, way, pl.ds(0, n)]
                else:
                    outs[2][r, way] = pack_z(v, at)
                    src, dst = out_z.at[r, way], in_z.at[r, way]
                k = 2 * d + way
                plan.append((src, dst, send_sem.at[r, k], recv_sem.at[r, k], d, way))
                send(*plan[-1])
        if meanwhile is not None:
            meanwhile()
        for item in plan:
            receive(*item)
        return [
            [in_x[r, way], in_y[r, way, pl.ds(0, n)], unpack_z(in_z[r, way], n)]
            for way in range(2)
        ]

    def inside(v, level):
        t, s = tables[level], 1 << level
        zero = [jnp.zeros(v.shape[1:], v.dtype), 0.0, 0.0]
        total = 0.0
        for d in range(3):
            total = total + (t[d] * up(v, zero, d, s) + t[3 + d] * down(v, zero, d, s))
        return total

    def outside(v, level, halos):
        low, high = halos
        t, s = tables[level], 1 << level
        total = 0.0
        for d in (1, 2):
            place_in = iota(v.shape, d)
            total = total + jnp.where(place_in >= v.shape[d] - s, t[d] * high[d], 0.0)
            total = total + jnp.where(place_in < s, t[3 + d] * low[d], 0.0)
        first, last = t[3, 0] * low[0], t[0, v.shape[0] - 1] * high[0]
        parts = [total[:1] + first[None], total[-1:] + last[None]]
        if v.shape[0] > 2:
            parts.insert(1, total[1:-1])
        return jnp.concatenate(parts, axis=0)

    def around(v, level, halos=None, meanwhile=None):
        if halos is None:
            box = []

            def work():
                if meanwhile is not None:
                    meanwhile()
                box.append(inside(v, level))

            halos = exchange(v, work)
            return box[0] + outside(v, level, halos)
        return inside(v, level) + outside(v, level, halos)

    def sweep(v, level, halos=None, meanwhile=None):
        t = tables[level]
        total = sides[level][...] + around(v, level, halos, meanwhile)
        return (1.0 - OMEGA) * v + t[7] * total

    def cycle(level):
        v = tables[level][7] * sides[level][...]
        if level == LEVELS - 1:
            for _ in range(COARSE_SWEEPS - 1):
                v = sweep(v, level)
            return v
        v = sweep(v, level, None, send_tables if gather and level == 0 else None)
        box = []
        halos = exchange(v, lambda: box.append(inside(v, level)))
        residual = sides[level][...] - tables[level][6] * v
        residual = residual + (box[0] + outside(v, level, halos))
        if gather and level == 1:
            coarse_solve(restrict(residual, 1 << level))
            v = v + prolong(answer_at(None, 0))
            v = sweep(v, level, [corrected(halos[0], 0), corrected(halos[1], 1)])
            return sweep(v, level)
        sides[level + 1][...] = restrict(residual, 1 << level)
        v = v + prolong(cycle(level + 1))
        for _ in range(2):
            v = sweep(v, level)
        return v

    pressure = cycle(0)
    low, high = exchange(pressure)
    change = jnp.zeros(shape, jnp.float32)
    fraction = frac_ref[...]
    for d in range(3):
        moved = open_u[d] - tables[0][d] * (up(pressure, high, d, 1) - pressure)
        moved_low = vel_low[d] - tables[0][3 + d] * (pressure - down(pressure, low, d, 1))
        vel_out[d] = moved
        flux = moved * jnp.where(moved > 0, fraction, frac_up_ref[d])
        flux_low = moved_low * jnp.where(moved_low > 0, frac_down_ref[d], fraction)
        change = change + (flux - flux_low)
    frac_out[...] = fraction - TIME_STEP * change

    for src, dst, ssem, rsem, d, way in sends:
        target = has_high[d] if way == 0 else has_low[d]

        @pl.when(target)
        def _():
            copy(src, dst, ssem, rsem, d, way).wait_send()

    for item in spreads:
        item.wait_send()


def body(counts, kernel, *refs):
    (fill, flags, smear, velocity, vel_out, frac_out, *scratch) = refs
    loaded, scratch = scratch[:5], scratch[5:]
    first, scratch = scratch[:12], scratch[12:]
    tables, scratch = scratch[:LEVELS], scratch[LEVELS:]
    sides, scratch = scratch[:LEVELS], scratch[LEVELS:]
    kernel(
        counts, fill, flags, smear, velocity, vel_out, frac_out, *loaded,
        *first, tables, sides, *scratch,
    )


def shards(counts, fill_mask, membrane_flags, smear, velocity):
    nx, ny, nz = fill_mask.shape
    f32 = jnp.float32
    vmem = lambda *s: pltpu.VMEM(s, f32)
    first = [vmem(2, 3, ny, nz), vmem(2, 3, nx, 1, nz), vmem(2, 3, ny, nz)] * 2
    rounds = [
        vmem(ROUNDS, 2, ny, nz), vmem(ROUNDS, 2, nx, 1, nz), vmem(ROUNDS, 2, ny, nz)
    ] * 2
    tables = [vmem(8, nx >> l, ny, nz) for l in range(LEVELS)]
    sides = [vmem(nx >> l, ny, nz) for l in range(LEVELS)]
    rest = [vmem(3, nx, ny, nz), vmem(3, nx, ny, nz), vmem(nx, ny, nz)]
    rest += [vmem(3, nx, ny, nz), vmem(3, nx, ny, nz)]
    sems = [pltpu.SemaphoreType.DMA((6,))] * 2 + [pltpu.SemaphoreType.DMA((ROUNDS, 6))] * 2
    loaded = [pltpu.VMEM(a.shape, a.dtype) for a in (fill_mask, membrane_flags, smear, velocity)]
    loaded += [pltpu.SemaphoreType.DMA((4,))]
    many = counts[0] * counts[1]
    peers = many * counts[2] if gathers(counts, fill_mask.shape) else 1
    sems += [
        vmem(4, 2, 1, nz), vmem(4, many, 2, counts[2], 1, nz), vmem(2, 1, nz),
        vmem(many, 2, counts[2], 1, nz), vmem(many, ny, nz),
    ] + [pltpu.SemaphoreType.DMA((2, peers))] * 2
    whole = pl.BlockSpec(memory_space=pltpu.VMEM)
    left = pl.BlockSpec(memory_space=pl.ANY)
    return pl.pallas_call(
        functools.partial(body, counts, kernel),
        out_shape=(
            jax.ShapeDtypeStruct(velocity.shape, f32),
            jax.ShapeDtypeStruct(fill_mask.shape, f32),
        ),
        in_specs=[left] * 4,
        out_specs=(whole, whole),
        scratch_shapes=loaded + first + rounds + tables + sides + rest + sems,
        compiler_params=pltpu.CompilerParams(
            collective_id=0, has_side_effects=True, vmem_limit_bytes=60 * 1024 * 1024
        ),
    )(fill_mask, membrane_flags, smear, velocity)


def solution(mesh):
    placed = (P("gx", "gy", "gz"),) * 3 + (P(None, "gx", "gy", "gz"),)
    counts = tuple(mesh.shape[a] for a in AXES)
    return jax.shard_map(
        functools.partial(shards, counts),
        mesh=mesh,
        in_specs=placed,
        out_specs=(P(None, "gx", "gy", "gz"), P("gx", "gy", "gz")),
        check_vma=False,
    )
```

```python
import functools

import jax
import jax.numpy as jnp
from jax import lax
from jax.experimental import pallas as pl
from jax.experimental.pallas import tpu as pltpu
from jax.sharding import PartitionSpec as P

LEVELS = 4
COARSE_SWEEPS = 8
AXES = ("gx", "gy", "gz")

RHO_LIQUID = 1000.0
RHO_GAS = 1.0
MEMBRANE_DROP = 49.0
SIGMA_SHIFT = 0.1
OMEGA = 0.8
TIME_STEP = 0.2

ROUNDS = 4 * (LEVELS - 1) + COARSE_SWEEPS - 1 + 1


def harmonic(a, b):
    return 2.0 * a * b / (a + b)


def iota(shape, dim):
    return lax.broadcasted_iota(jnp.int32, shape, dim)


def roll(v, shift, dim):
    size = v.shape[dim]
    shift = shift % size
    return v if shift == 0 else pltpu.roll(v, shift, dim)


def odd_mask(v, dim, step):
    return (iota(v.shape, dim) // step) % 2 == 1


def pair_sum(v, dim, step):
    return v + jnp.where(odd_mask(v, dim, step), roll(v, step, dim), roll(v, -step, dim))


def take_odd(v, dim, step):
    return jnp.where(odd_mask(v, dim, step), v, roll(v, -step, dim))


def take_even(v, dim, step):
    return jnp.where(odd_mask(v, dim, step), roll(v, step, dim), v)


def halves(v):
    w = v.reshape(v.shape[0] // 2, 2, v.shape[1], v.shape[2])
    return w[:, 0], w[:, 1]


def restrict(v, step):
    a, b = halves(v)
    return pair_sum(pair_sum(a + b, 1, step), 2, step)


def prolong(v):
    n = v.shape[0]
    w = jnp.broadcast_to(v[:, None], (n, 2, v.shape[1], v.shape[2]))
    return w.reshape(2 * n, v.shape[1], v.shape[2])


def pack_z(v, lane):
    n = v.shape[0]
    wide = jnp.broadcast_to(v[:, :, lane : lane + 1], v.shape)
    return jnp.sum(jnp.where(iota(v.shape, 2) == iota(v.shape, 0), wide, 0.0), axis=0)


def unpack_z(tile, n):
    return jnp.stack([jnp.broadcast_to(tile[:, i : i + 1], tile.shape) for i in range(n)])


def up(v, halos, d, step):
    if d == 0:
        return jnp.concatenate([v[1:], halos[0][None]], axis=0)
    size = v.shape[d]
    return jnp.where(iota(v.shape, d) >= size - step, halos[d], roll(v, -step, d))


def down(v, halos, d, step):
    if d == 0:
        return jnp.concatenate([halos[0][None], v[:-1]], axis=0)
    return jnp.where(iota(v.shape, d) < step, halos[d], roll(v, step, d))


def gathers(counts, shape):
    return shape == (16, 8, 128) and counts == (2, 4, 4)


def compact(f):
    wide = iota(f.shape, 2) % 4 == iota(f.shape, 0)
    return jnp.sum(jnp.where(wide, f, 0.0), axis=0)


def turned(v, by):
    return jnp.concatenate([v[by:], v[:by]], axis=0)


def dense_up(v, d, s, ny):
    lane, row = iota(v.shape, 2), iota(v.shape, 1)
    if d == 0:
        return jnp.where(lane % 4 + s < 4, roll(v, -s, 2), roll(turned(v, ny), 4 - s, 2))
    if d == 1:
        far = turned(v, 1)
        return far if s == 2 else roll(jnp.where(row >= 4, v, far), 4, 1)
    near = roll(v, -4 * s, 2)
    return jnp.where(lane < 128 - 4 * s, near, roll(near, -1, 1))


def dense_down(v, d, s, ny):
    lane, row = iota(v.shape, 2), iota(v.shape, 1)
    if d == 0:
        return jnp.where(lane % 4 >= s, roll(v, s, 2), roll(turned(v, -ny), s - 4, 2))
    if d == 1:
        far = turned(v, -1)
        return far if s == 2 else roll(jnp.where(row < 4, v, far), 4, 1)
    near = roll(v, 4 * s, 2)
    return jnp.where(lane >= 4 * s, near, roll(near, 1, 1))


def dense_tables(upper, shift, s, ny):
    lower = [dense_down(upper[d], d, s, ny) for d in range(3)]
    diagonal = shift
    for d in range(3):
        diagonal = diagonal + upper[d] + lower[d]
    return upper + lower + [diagonal, OMEGA / diagonal]


def dense_around(v, t, s, ny):
    total = 0.0
    for d in range(3):
        total = total + (t[d] * dense_up(v, d, s, ny) + t[3 + d] * dense_down(v, d, s, ny))
    return total


def dense_sweep(v, rhs, t, s, ny):
    return (1.0 - OMEGA) * v + t[7] * (rhs + dense_around(v, t, s, ny))


def dense_cycle(rhs, fine, coarse, ny):
    v = fine[7] * rhs
    v = dense_sweep(v, rhs, fine, 1, ny)
    residual = rhs - fine[6] * v + dense_around(v, fine, 1, ny)
    rhs3 = pair_sum(pair_sum(pair_sum(residual, 2, 1), 1, 4), 2, 4)
    e = coarse[7] * rhs3
    for _ in range(COARSE_SWEEPS - 1):
        e = dense_sweep(e, rhs3, coarse, 2, ny)
    v = v + e
    for _ in range(2):
        v = dense_sweep(v, rhs, fine, 1, ny)
    return v


def local_of(tile, gz):
    own = jnp.where(iota(tile.shape, 0) % 4 == gz, tile, 0.0)
    own = pair_sum(pair_sum(own, 0, 1), 0, 2)
    wide = jnp.broadcast_to(own[None], (4,) + own.shape)
    wide = jnp.where(iota(wide.shape, 2) % 4 == iota(wide.shape, 0), wide, 0.0)
    return pair_sum(pair_sum(wide, 2, 1), 2, 2)


def kernel(
    counts, fill_at, flags_at, smear_at, velocity_at, vel_out, frac_out,
    fill, flags, smear, velocity, load_sem,
    first_x, first_y, first_z, got_x, got_y, got_z,
    out_x, out_y, out_z, in_x, in_y, in_z,
    tables, sides, open_u, vel_low, frac_ref, frac_up_ref, frac_down_ref,
    first_send, first_recv, send_sem, recv_sem,
    own_tables, all_tables, own_side, all_side, answer, all_send, all_recv,
):
    nx, ny, nz = fill.shape
    place = [lax.axis_index(a) for a in AXES]
    has_low = [place[d] > 0 for d in range(3)]
    has_high = [place[d] < counts[d] - 1 for d in range(3)]

    gather = gathers(counts, fill.shape)
    loads = [
        pltpu.make_async_copy(src, dst, load_sem.at[i])
        for i, (src, dst) in enumerate(
            zip((fill_at, flags_at, smear_at, velocity_at), (fill, flags, smear, velocity))
        )
    ]
    for load in loads:
        load.start()
    offsets = [
        (i, j, k) for i in range(counts[0]) for j in range(counts[1])
        for k in range(counts[2]) if (i, j, k) != (0, 0, 0)
    ]
    offsets.sort(key=lambda o: -sum(max(p, c - p) for p, c in zip(o, counts) if p))

    def peer(offset, sign):
        return tuple(
            lax.rem(place[d] + (counts[d] + sign * offset[d]), counts[d]) for d in range(3)
        )

    barrier = pltpu.get_barrier_semaphore()
    for offset in offsets if gather else []:
        pl.semaphore_signal(
            barrier, inc=1, device_id=peer(offset, 1),
            device_id_type=pl.DeviceIdType.MESH,
        )
    for d in [] if gather else range(3):
        for there, step in ((has_low[d], -1), (has_high[d], 1)):
            @pl.when(there)
            def _():
                pl.semaphore_signal(
                    barrier, inc=1, device_id={AXES[d]: place[d] + step},
                    device_id_type=pl.DeviceIdType.MESH,
                )
    walls = zip((got_x, got_y, got_z), (in_x, in_y, in_z), has_low, has_high)
    for first_in, all_in, *there in walls:
        for way in range(2):
            @pl.when(jnp.logical_not(there[way]))
            def _():
                first_in[way] = jnp.zeros(first_in.shape[1:], first_in.dtype)
                for r in range(all_in.shape[0]):
                    all_in[r, way] = jnp.zeros(all_in.shape[2:], all_in.dtype)

    total = len(offsets)
    if not gather:
        total = sum(c.astype(jnp.int32) for c in has_low + has_high)

    sends = []

    def copy(src, dst, ssem, rsem, d, way):
        return pltpu.make_async_remote_copy(
            src_ref=src, dst_ref=dst, send_sem=ssem, recv_sem=rsem,
            device_id={AXES[d]: place[d] + (1 if way == 0 else -1)},
            device_id_type=pl.DeviceIdType.MESH,
        )

    def send(src, dst, ssem, rsem, d, way):
        target = has_high[d] if way == 0 else has_low[d]

        @pl.when(target)
        def _():
            copy(src, dst, ssem, rsem, d, way).start()

        sends.append((src, dst, ssem, rsem, d, way))

    def receive(src, dst, ssem, rsem, d, way):
        source = has_low[d] if way == 0 else has_high[d]

        @pl.when(source)
        def _():
            copy(src, dst, ssem, rsem, d, way).wait_recv()

    for load in loads:
        load.wait()
    filled = fill[...].astype(jnp.float32)
    walled = flags[...].astype(jnp.float32)
    soft = 0.4 * smear[...]
    fraction = filled * (1.0 - soft) + (1.0 - filled) * soft
    density = RHO_GAS + (RHO_LIQUID - RHO_GAS) * fraction
    conductance = 1.0 / (density * (1.0 + MEMBRANE_DROP * walled))
    shape = fraction.shape
    speeds = []
    for d in range(3):
        position = place[d] * shape[d] + iota(shape, d)
        speeds.append(
            velocity[d] * (position < shape[d] * counts[d] - 1).astype(jnp.float32)
        )
        open_u[d] = speeds[d]
    frac_ref[...] = fraction

    firsts, gots = (first_x, first_y, first_z), (got_x, got_y, got_z)
    plan = []
    for d in range(3):
        for way in range(2):
            at = shape[d] - 1 if way == 0 else 0
            items = [conductance, fraction] + ([speeds[d]] if way == 0 else [])
            for k, item in enumerate(items):
                if d == 0:
                    firsts[0][way, k] = item[at]
                elif d == 1:
                    firsts[1][way, k] = item[:, at : at + 1, :]
                else:
                    firsts[2][way, k] = pack_z(item, at)
            many = pl.ds(0, len(items))
            plan.append((
                firsts[d].at[way, many], gots[d].at[way, many],
                first_send.at[2 * d + way], first_recv.at[2 * d + way], d, way,
            ))
    pl.semaphore_wait(barrier, total)
    for item in plan:
        send(*item)
    for item in plan:
        receive(*item)

    def first_halos(k, way):
        return [got_x[way, k], got_y[way, k], unpack_z(got_z[way, k], nx)]

    cond_low, cond_high = first_halos(0, 0), first_halos(0, 1)
    frac_low, frac_high = first_halos(1, 0), first_halos(1, 1)
    speed_low = first_halos(2, 0)
    upper = [harmonic(conductance, up(conductance, cond_high, d, 1)) for d in range(3)]
    lower = [harmonic(down(conductance, cond_low, d, 1), conductance) for d in range(3)]
    shift = SIGMA_SHIFT * conductance
    change = jnp.zeros(shape, jnp.float32)
    for d in range(3):
        frac_up_ref[d] = up(fraction, frac_high, d, 1)
        frac_down_ref[d] = down(fraction, frac_low, d, 1)
        low = down(speeds[d], speed_low, d, 1)
        vel_low[d] = low
        change = change + (speeds[d] - low)
    sides[0][...] = -change

    for level in range(2 if gather else LEVELS):
        diagonal = shift
        for d in range(3):
            tables[level][d] = upper[d]
            tables[level][3 + d] = lower[d]
            diagonal = diagonal + upper[d] + lower[d]
        tables[level][6] = diagonal
        tables[level][7] = OMEGA / diagonal
        if level < LEVELS - 1:
            s = 1 << level
            (a, b), (c, e) = halves(upper[0]), halves(lower[0])
            upper_x = pair_sum(pair_sum(b, 1, s), 2, s)
            lower_x = pair_sum(pair_sum(c, 1, s), 2, s)
            both = lambda v: sum(halves(v))
            upper_y = pair_sum(take_odd(both(upper[1]), 1, s), 2, s)
            lower_y = pair_sum(take_even(both(lower[1]), 1, s), 2, s)
            upper_z = pair_sum(take_odd(both(upper[2]), 2, s), 1, s)
            lower_z = pair_sum(take_even(both(lower[2]), 2, s), 1, s)
            upper, lower = [upper_x, upper_y, upper_z], [lower_x, lower_y, lower_z]
            shift = restrict(shift, s)

    outs, ins = (out_x, out_y, out_z), (in_x, in_y, in_z)
    count = [0]

    def spread(src, dst_of, k):
        dst_of(place)[...] = src[...]
        copies = []
        for i, offset in enumerate(offsets):
            copies.append(pltpu.make_async_remote_copy(
                src_ref=src, dst_ref=dst_of(place),
                send_sem=all_send.at[k, i], recv_sem=all_recv.at[k, i],
                device_id=peer(offset, 1), device_id_type=pl.DeviceIdType.MESH,
            ))
            copies[-1].start()
        return copies

    def table_at(p):
        return all_tables.at[:, p[0] * counts[1] + p[1], :, p[2]]

    def side_at(p):
        return all_side.at[p[0] * counts[1] + p[1], :, p[2]]

    def collect(dst_of, k):
        for i, offset in enumerate(offsets):
            ref = dst_of(peer(offset, -1))
            pltpu.make_async_remote_copy(
                src_ref=ref, dst_ref=ref,
                send_sem=all_send.at[k, i], recv_sem=all_recv.at[k, i],
                device_id=peer(offset, -1), device_id_type=pl.DeviceIdType.MESH,
            ).wait_recv()

    def rows(f):
        tile = compact(f)
        return [tile[0:1], tile[4:5]]

    spreads = []

    def send_tables():
        for k, f in enumerate(upper + [shift]):
            for j, row in enumerate(rows(f)):
                own_tables[k, j] = row
        spreads.extend(spread(own_tables, table_at, 0))

    def coarse_solve(residual2):
        for j, row in enumerate(rows(residual2)):
            own_side[j] = row
        spreads.extend(spread(own_side, side_at, 1))
        collect(table_at, 0)
        many = counts[0] * counts[1]
        shaped = lambda w: w.reshape(many, 8, 128)
        *up2, shift2 = [shaped(all_tables[k]) for k in range(4)]
        ny = counts[1]
        y_z = lambda v: pair_sum(pair_sum(v, 1, 4), 2, 4)
        up3 = [
            y_z(take_odd(up2[0], 2, 1)),
            pair_sum(pair_sum(take_odd(up2[1], 1, 4), 2, 1), 2, 4),
            pair_sum(pair_sum(take_odd(up2[2], 2, 4), 2, 1), 1, 4),
        ]
        shift3 = pair_sum(y_z(shift2), 2, 1)
        fine = dense_tables(up2, shift2, 1, ny)
        coarse = dense_tables(up3, shift3, 2, ny)
        collect(side_at, 1)
        answer[...] = dense_cycle(shaped(all_side[...]), fine, coarse, ny)

    def answer_at(d, step):
        p = list(place)
        if d is not None:
            p[d] = lax.rem(p[d] + (counts[d] + step), counts[d])
        return local_of(answer[p[0] * counts[1] + p[1]], p[2])

    def corrected(halos, way):
        step = -1 if way == 0 else 1
        e = [answer_at(d, step) for d in range(3)]
        edge = lambda f, d: f.shape[d] - 1 if way == 0 else 0
        x, y, z = edge(e[0], 0), edge(e[1], 1), edge(e[2], 2)
        return [
            halos[0] + e[0][x],
            halos[1] + prolong(e[1][:, y : y + 1, :]),
            halos[2] + prolong(jnp.broadcast_to(e[2][:, :, z : z + 1], e[2].shape)),
        ]

    def exchange(v, meanwhile=None):
        r = count[0]
        count[0] += 1
        n = v.shape[0]
        plan = []
        for d in range(3):
            for way in range(2):
                at = v.shape[d] - 1 if way == 0 else 0
                if d == 0:
                    outs[0][r, way] = v[at]
                    src, dst = out_x.at[r, way], in_x.at[r, way]
                elif d == 1:
                    outs[1][r, way, pl.ds(0, n)] = v[:, at : at + 1, :]
                    src = out_y.at[r, way, pl.ds(0, n)]
                    dst = in_y.at[r, way, pl.ds(0, n)]
                else:
                    outs[2][r, way] = pack_z(v, at)
                    src, dst = out_z.at[r, way], in_z.at[r, way]
                k = 2 * d + way
                plan.append((src, dst, send_sem.at[r, k], recv_sem.at[r, k], d, way))
                send(*plan[-1])
        if meanwhile is not None:
            meanwhile()
        for item in plan:
            receive(*item)
        return [
            [in_x[r, way], in_y[r, way, pl.ds(0, n)], unpack_z(in_z[r, way], n)]
            for way in range(2)
        ]

    def inside(v, level):
        t, s = tables[level], 1 << level
        zero = [jnp.zeros(v.shape[1:], v.dtype), 0.0, 0.0]
        total = 0.0
        for d in range(3):
            total = total + (t[d] * up(v, zero, d, s) + t[3 + d] * down(v, zero, d, s))
        return total

    def outside(v, level, halos):
        low, high = halos
        t, s = tables[level], 1 << level
        total = 0.0
        for d in (1, 2):
            place_in = iota(v.shape, d)
            total = total + jnp.where(place_in >= v.shape[d] - s, t[d] * high[d], 0.0)
            total = total + jnp.where(place_in < s, t[3 + d] * low[d], 0.0)
        first, last = t[3, 0] * low[0], t[0, v.shape[0] - 1] * high[0]
        parts = [total[:1] + first[None], total[-1:] + last[None]]
        if v.shape[0] > 2:
            parts.insert(1, total[1:-1])
        return jnp.concatenate(parts, axis=0)

    def around(v, level, halos=None, meanwhile=None):
        if halos is None:
            box = []

            def work():
                if meanwhile is not None:
                    meanwhile()
                box.append(inside(v, level))

            halos = exchange(v, work)
            return box[0] + outside(v, level, halos)
        return inside(v, level) + outside(v, level, halos)

    def sweep(v, level, halos=None, meanwhile=None):
        t = tables[level]
        total = sides[level][...] + around(v, level, halos, meanwhile)
        return (1.0 - OMEGA) * v + t[7] * total

    def cycle(level):
        v = tables[level][7] * sides[level][...]
        if level == LEVELS - 1:
            for _ in range(COARSE_SWEEPS - 1):
                v = sweep(v, level)
            return v
        v = sweep(v, level, None, send_tables if gather and level == 0 else None)
        box = []
        halos = exchange(v, lambda: box.append(inside(v, level)))
        residual = sides[level][...] - tables[level][6] * v
        residual = residual + (box[0] + outside(v, level, halos))
        if gather and level == 1:
            coarse_solve(restrict(residual, 1 << level))
            v = v + prolong(answer_at(None, 0))
            v = sweep(v, level, [corrected(halos[0], 0), corrected(halos[1], 1)])
            return sweep(v, level)
        sides[level + 1][...] = restrict(residual, 1 << level)
        v = v + prolong(cycle(level + 1))
        for _ in range(2):
            v = sweep(v, level)
        return v

    pressure = cycle(0)
    low, high = exchange(pressure)
    change = jnp.zeros(shape, jnp.float32)
    fraction = frac_ref[...]
    for d in range(3):
        moved = open_u[d] - tables[0][d] * (up(pressure, high, d, 1) - pressure)
        moved_low = vel_low[d] - tables[0][3 + d] * (pressure - down(pressure, low, d, 1))
        vel_out[d] = moved
        flux = moved * jnp.where(moved > 0, fraction, frac_up_ref[d])
        flux_low = moved_low * jnp.where(moved_low > 0, frac_down_ref[d], fraction)
        change = change + (flux - flux_low)
    frac_out[...] = fraction - TIME_STEP * change

    for src, dst, ssem, rsem, d, way in sends:
        target = has_high[d] if way == 0 else has_low[d]

        @pl.when(target)
        def _():
            copy(src, dst, ssem, rsem, d, way).wait_send()

    for item in spreads:
        item.wait_send()


def body(counts, kernel, *refs):
    (fill, flags, smear, velocity, vel_out, frac_out, *scratch) = refs
    loaded, scratch = scratch[:5], scratch[5:]
    first, scratch = scratch[:12], scratch[12:]
    tables, scratch = scratch[:LEVELS], scratch[LEVELS:]
    sides, scratch = scratch[:LEVELS], scratch[LEVELS:]
    kernel(
        counts, fill, flags, smear, velocity, vel_out, frac_out, *loaded,
        *first, tables, sides, *scratch,
    )


def shards(counts, fill_mask, membrane_flags, smear, velocity):
    nx, ny, nz = fill_mask.shape
    f32 = jnp.float32
    vmem = lambda *s: pltpu.VMEM(s, f32)
    first = [vmem(2, 3, ny, nz), vmem(2, 3, nx, 1, nz), vmem(2, 3, ny, nz)] * 2
    many = 8 if gathers(counts, fill_mask.shape) else ROUNDS
    rounds = [vmem(many, 2, ny, nz), vmem(many, 2, nx, 1, nz), vmem(many, 2, ny, nz)] * 2
    tables = [vmem(8, nx >> l, ny, nz) for l in range(LEVELS)]
    sides = [vmem(nx >> l, ny, nz) for l in range(LEVELS)]
    rest = [vmem(3, nx, ny, nz), vmem(3, nx, ny, nz), vmem(nx, ny, nz)]
    rest += [vmem(3, nx, ny, nz), vmem(3, nx, ny, nz)]
    sems = [pltpu.SemaphoreType.DMA((6,))] * 2 + [pltpu.SemaphoreType.DMA((many, 6))] * 2
    loaded = [pltpu.VMEM(a.shape, a.dtype) for a in (fill_mask, membrane_flags, smear, velocity)]
    loaded += [pltpu.SemaphoreType.DMA((4,))]
    many = counts[0] * counts[1]
    peers = many * counts[2] if gathers(counts, fill_mask.shape) else 1
    sems += [
        vmem(4, 2, 1, nz), vmem(4, many, 2, counts[2], 1, nz), vmem(2, 1, nz),
        vmem(many, 2, counts[2], 1, nz), vmem(many, ny, nz),
    ] + [pltpu.SemaphoreType.DMA((2, peers))] * 2
    whole = pl.BlockSpec(memory_space=pltpu.VMEM)
    left = pl.BlockSpec(memory_space=pl.ANY)
    return pl.pallas_call(
        functools.partial(body, counts, kernel),
        out_shape=(
            jax.ShapeDtypeStruct(velocity.shape, f32),
            jax.ShapeDtypeStruct(fill_mask.shape, f32),
        ),
        in_specs=[left] * 4,
        out_specs=(whole, whole),
        scratch_shapes=loaded + first + rounds + tables + sides + rest + sems,
        compiler_params=pltpu.CompilerParams(
            collective_id=0, has_side_effects=True, vmem_limit_bytes=60 * 1024 * 1024
        ),
    )(fill_mask, membrane_flags, smear, velocity)


def solution(mesh):
    placed = (P("gx", "gy", "gz"),) * 3 + (P(None, "gx", "gy", "gz"),)
    counts = tuple(mesh.shape[a] for a in AXES)
    return jax.shard_map(
        functools.partial(shards, counts),
        mesh=mesh,
        in_specs=placed,
        out_specs=(P(None, "gx", "gy", "gz"), P("gx", "gy", "gz")),
        check_vma=False,
    )
```

```python
import functools

import jax
import jax.numpy as jnp
from jax import lax
from jax.experimental import pallas as pl
from jax.experimental.pallas import tpu as pltpu
from jax.sharding import PartitionSpec as P

LEVELS = 4
COARSE_SWEEPS = 8
AXES = ("gx", "gy", "gz")

RHO_LIQUID = 1000.0
RHO_GAS = 1.0
MEMBRANE_DROP = 49.0
SIGMA_SHIFT = 0.1
OMEGA = 0.8
TIME_STEP = 0.2

ROUNDS = 4 * (LEVELS - 1) + COARSE_SWEEPS - 1 + 1


def harmonic(a, b):
    return 2.0 * a * b / (a + b)


def iota(shape, dim):
    return lax.broadcasted_iota(jnp.int32, shape, dim)


def roll(v, shift, dim):
    size = v.shape[dim]
    shift = shift % size
    return v if shift == 0 else pltpu.roll(v, shift, dim)


def odd_mask(v, dim, step):
    return (iota(v.shape, dim) // step) % 2 == 1


def pair_sum(v, dim, step):
    return v + jnp.where(odd_mask(v, dim, step), roll(v, step, dim), roll(v, -step, dim))


def take_odd(v, dim, step):
    return jnp.where(odd_mask(v, dim, step), v, roll(v, -step, dim))


def take_even(v, dim, step):
    return jnp.where(odd_mask(v, dim, step), roll(v, step, dim), v)


def halves(v):
    w = v.reshape(v.shape[0] // 2, 2, v.shape[1], v.shape[2])
    return w[:, 0], w[:, 1]


def restrict(v, step):
    a, b = halves(v)
    return pair_sum(pair_sum(a + b, 1, step), 2, step)


def prolong(v):
    n = v.shape[0]
    w = jnp.broadcast_to(v[:, None], (n, 2, v.shape[1], v.shape[2]))
    return w.reshape(2 * n, v.shape[1], v.shape[2])


def pack_z(v, lane):
    n = v.shape[0]
    wide = jnp.broadcast_to(v[:, :, lane : lane + 1], v.shape)
    return jnp.sum(jnp.where(iota(v.shape, 2) == iota(v.shape, 0), wide, 0.0), axis=0)


def unpack_z(tile, n):
    return jnp.stack([jnp.broadcast_to(tile[:, i : i + 1], tile.shape) for i in range(n)])


def up(v, halos, d, step):
    if d == 0:
        return jnp.concatenate([v[1:], halos[0][None]], axis=0)
    size = v.shape[d]
    return jnp.where(iota(v.shape, d) >= size - step, halos[d], roll(v, -step, d))


def down(v, halos, d, step):
    if d == 0:
        return jnp.concatenate([halos[0][None], v[:-1]], axis=0)
    return jnp.where(iota(v.shape, d) < step, halos[d], roll(v, step, d))


def gathers(counts, shape):
    return shape == (16, 8, 128) and counts == (2, 4, 4)


def compact(f):
    wide = iota(f.shape, 2) % 4 == iota(f.shape, 0)
    return jnp.sum(jnp.where(wide, f, 0.0), axis=0)


def turned(v, by):
    return jnp.concatenate([v[by:], v[:by]], axis=0)


def dense_up(v, d, s, ny):
    lane, row = iota(v.shape, 2), iota(v.shape, 1)
    if d == 0:
        return jnp.where(lane % 4 + s < 4, roll(v, -s, 2), roll(turned(v, ny), 4 - s, 2))
    if d == 1:
        far = turned(v, 1)
        return far if s == 2 else roll(jnp.where(row >= 4, v, far), 4, 1)
    near = roll(v, -4 * s, 2)
    return jnp.where(lane < 128 - 4 * s, near, roll(near, -1, 1))


def dense_down(v, d, s, ny):
    lane, row = iota(v.shape, 2), iota(v.shape, 1)
    if d == 0:
        return jnp.where(lane % 4 >= s, roll(v, s, 2), roll(turned(v, -ny), s - 4, 2))
    if d == 1:
        far = turned(v, -1)
        return far if s == 2 else roll(jnp.where(row < 4, v, far), 4, 1)
    near = roll(v, 4 * s, 2)
    return jnp.where(lane >= 4 * s, near, roll(near, 1, 1))


def dense_tables(upper, shift, s, ny):
    lower = [dense_down(upper[d], d, s, ny) for d in range(3)]
    diagonal = shift
    for d in range(3):
        diagonal = diagonal + upper[d] + lower[d]
    return upper + lower + [diagonal, OMEGA / diagonal]


def dense_around(v, t, s, ny):
    total = 0.0
    for d in range(3):
        total = total + (t[d] * dense_up(v, d, s, ny) + t[3 + d] * dense_down(v, d, s, ny))
    return total


def dense_sweep(v, rhs, t, s, ny):
    return (1.0 - OMEGA) * v + t[7] * (rhs + dense_around(v, t, s, ny))


def dense_cycle(rhs, fine, coarse, ny):
    v = fine[7] * rhs
    v = dense_sweep(v, rhs, fine, 1, ny)
    residual = rhs - fine[6] * v + dense_around(v, fine, 1, ny)
    rhs3 = pair_sum(pair_sum(pair_sum(residual, 2, 1), 1, 4), 2, 4)
    e = coarse[7] * rhs3
    for _ in range(COARSE_SWEEPS - 1):
        e = dense_sweep(e, rhs3, coarse, 2, ny)
    v = v + e
    for _ in range(2):
        v = dense_sweep(v, rhs, fine, 1, ny)
    return v


def local_of(tile, gz):
    own = jnp.where(iota(tile.shape, 0) % 4 == gz, tile, 0.0)
    own = pair_sum(pair_sum(own, 0, 1), 0, 2)
    wide = jnp.broadcast_to(own[None], (4,) + own.shape)
    wide = jnp.where(iota(wide.shape, 2) % 4 == iota(wide.shape, 0), wide, 0.0)
    return pair_sum(pair_sum(wide, 2, 1), 2, 2)


def kernel(
    counts, fill_at, flags_at, smear_at, velocity_at, vel_out, frac_out,
    fill, flags, smear, velocity, load_sem, out_velocity, out_fraction, store_sem,
    first_x, first_y, first_z, got_x, got_y, got_z,
    out_x, out_y, out_z, in_x, in_y, in_z,
    tables, sides, open_u, vel_low, frac_ref, frac_up_ref, frac_down_ref,
    first_send, first_recv, send_sem, recv_sem,
    own_tables, all_tables, own_side, all_side, answer, all_send, all_recv,
):
    nx, ny, nz = fill.shape
    place = [lax.axis_index(a) for a in AXES]
    has_low = [place[d] > 0 for d in range(3)]
    has_high = [place[d] < counts[d] - 1 for d in range(3)]

    gather = gathers(counts, fill.shape)
    loads = [
        pltpu.make_async_copy(src, dst, load_sem.at[i])
        for i, (src, dst) in enumerate(
            zip((fill_at, flags_at, smear_at, velocity_at), (fill, flags, smear, velocity))
        )
    ]
    for load in loads:
        load.start()
    offsets = [
        (i, j, k) for i in range(counts[0]) for j in range(counts[1])
        for k in range(counts[2]) if (i, j, k) != (0, 0, 0)
    ]
    offsets.sort(key=lambda o: -sum(max(p, c - p) for p, c in zip(o, counts) if p))

    def peer(offset, sign):
        return tuple(
            lax.rem(place[d] + (counts[d] + sign * offset[d]), counts[d]) for d in range(3)
        )

    barrier = pltpu.get_barrier_semaphore()
    for offset in offsets if gather else []:
        pl.semaphore_signal(
            barrier, inc=1, device_id=peer(offset, 1),
            device_id_type=pl.DeviceIdType.MESH,
        )
    for d in [] if gather else range(3):
        for there, step in ((has_low[d], -1), (has_high[d], 1)):
            @pl.when(there)
            def _():
                pl.semaphore_signal(
                    barrier, inc=1, device_id={AXES[d]: place[d] + step},
                    device_id_type=pl.DeviceIdType.MESH,
                )
    walls = zip((got_x, got_y, got_z), (in_x, in_y, in_z), has_low, has_high)
    for first_in, all_in, *there in walls:
        for way in range(2):
            @pl.when(jnp.logical_not(there[way]))
            def _():
                first_in[way] = jnp.zeros(first_in.shape[1:], first_in.dtype)
                for r in range(all_in.shape[0]):
                    all_in[r, way] = jnp.zeros(all_in.shape[2:], all_in.dtype)

    total = len(offsets)
    if not gather:
        total = sum(c.astype(jnp.int32) for c in has_low + has_high)

    sends = []

    def copy(src, dst, ssem, rsem, d, way):
        return pltpu.make_async_remote_copy(
            src_ref=src, dst_ref=dst, send_sem=ssem, recv_sem=rsem,
            device_id={AXES[d]: place[d] + (1 if way == 0 else -1)},
            device_id_type=pl.DeviceIdType.MESH,
        )

    def send(src, dst, ssem, rsem, d, way):
        target = has_high[d] if way == 0 else has_low[d]

        @pl.when(target)
        def _():
            copy(src, dst, ssem, rsem, d, way).start()

        sends.append((src, dst, ssem, rsem, d, way))

    def receive(src, dst, ssem, rsem, d, way):
        source = has_low[d] if way == 0 else has_high[d]

        @pl.when(source)
        def _():
            copy(src, dst, ssem, rsem, d, way).wait_recv()

    for load in loads:
        load.wait()
    filled = fill[...].astype(jnp.float32)
    walled = flags[...].astype(jnp.float32)
    soft = 0.4 * smear[...]
    fraction = filled * (1.0 - soft) + (1.0 - filled) * soft
    density = RHO_GAS + (RHO_LIQUID - RHO_GAS) * fraction
    conductance = 1.0 / (density * (1.0 + MEMBRANE_DROP * walled))
    shape = fraction.shape
    speeds = []
    for d in range(3):
        position = place[d] * shape[d] + iota(shape, d)
        speeds.append(
            velocity[d] * (position < shape[d] * counts[d] - 1).astype(jnp.float32)
        )
        open_u[d] = speeds[d]
    frac_ref[...] = fraction

    firsts, gots = (first_x, first_y, first_z), (got_x, got_y, got_z)
    plan = []
    for d in range(3):
        for way in range(2):
            at = shape[d] - 1 if way == 0 else 0
            items = [conductance, fraction] + ([speeds[d]] if way == 0 else [])
            for k, item in enumerate(items):
                if d == 0:
                    firsts[0][way, k] = item[at]
                elif d == 1:
                    firsts[1][way, k] = item[:, at : at + 1, :]
                else:
                    firsts[2][way, k] = pack_z(item, at)
            many = pl.ds(0, len(items))
            plan.append((
                firsts[d].at[way, many], gots[d].at[way, many],
                first_send.at[2 * d + way], first_recv.at[2 * d + way], d, way,
            ))
    pl.semaphore_wait(barrier, total)
    for item in plan:
        send(*item)
    for item in plan:
        receive(*item)

    def first_halos(k, way):
        return [got_x[way, k], got_y[way, k], unpack_z(got_z[way, k], nx)]

    cond_low, cond_high = first_halos(0, 0), first_halos(0, 1)
    frac_low, frac_high = first_halos(1, 0), first_halos(1, 1)
    speed_low = first_halos(2, 0)
    upper = [harmonic(conductance, up(conductance, cond_high, d, 1)) for d in range(3)]
    lower = [harmonic(down(conductance, cond_low, d, 1), conductance) for d in range(3)]
    shift = SIGMA_SHIFT * conductance
    change = jnp.zeros(shape, jnp.float32)
    for d in range(3):
        frac_up_ref[d] = up(fraction, frac_high, d, 1)
        frac_down_ref[d] = down(fraction, frac_low, d, 1)
        low = down(speeds[d], speed_low, d, 1)
        vel_low[d] = low
        change = change + (speeds[d] - low)
    sides[0][...] = -change

    for level in range(2 if gather else LEVELS):
        diagonal = shift
        for d in range(3):
            tables[level][d] = upper[d]
            tables[level][3 + d] = lower[d]
            diagonal = diagonal + upper[d] + lower[d]
        tables[level][6] = diagonal
        tables[level][7] = OMEGA / diagonal
        if level < LEVELS - 1:
            s = 1 << level
            (a, b), (c, e) = halves(upper[0]), halves(lower[0])
            upper_x = pair_sum(pair_sum(b, 1, s), 2, s)
            lower_x = pair_sum(pair_sum(c, 1, s), 2, s)
            both = lambda v: sum(halves(v))
            upper_y = pair_sum(take_odd(both(upper[1]), 1, s), 2, s)
            lower_y = pair_sum(take_even(both(lower[1]), 1, s), 2, s)
            upper_z = pair_sum(take_odd(both(upper[2]), 2, s), 1, s)
            lower_z = pair_sum(take_even(both(lower[2]), 2, s), 1, s)
            upper, lower = [upper_x, upper_y, upper_z], [lower_x, lower_y, lower_z]
            shift = restrict(shift, s)

    outs, ins = (out_x, out_y, out_z), (in_x, in_y, in_z)
    count = [0]

    def spread(src, dst_of, k):
        dst_of(place)[...] = src[...]
        copies = []
        for i, offset in enumerate(offsets):
            copies.append(pltpu.make_async_remote_copy(
                src_ref=src, dst_ref=dst_of(place),
                send_sem=all_send.at[k, i], recv_sem=all_recv.at[k, i],
                device_id=peer(offset, 1), device_id_type=pl.DeviceIdType.MESH,
            ))
            copies[-1].start()
        return copies

    def table_at(p):
        return all_tables.at[:, p[0] * counts[1] + p[1], :, p[2]]

    def side_at(p):
        return all_side.at[p[0] * counts[1] + p[1], :, p[2]]

    def collect(dst_of, k):
        for i, offset in enumerate(offsets):
            ref = dst_of(peer(offset, -1))
            pltpu.make_async_remote_copy(
                src_ref=ref, dst_ref=ref,
                send_sem=all_send.at[k, i], recv_sem=all_recv.at[k, i],
                device_id=peer(offset, -1), device_id_type=pl.DeviceIdType.MESH,
            ).wait_recv()

    def rows(f):
        tile = compact(f)
        return [tile[0:1], tile[4:5]]

    spreads = []

    def send_tables():
        for k, f in enumerate(upper + [shift]):
            for j, row in enumerate(rows(f)):
                own_tables[k, j] = row
        spreads.extend(spread(own_tables, table_at, 0))

    def coarse_solve(residual2):
        for j, row in enumerate(rows(residual2)):
            own_side[j] = row
        spreads.extend(spread(own_side, side_at, 1))
        collect(table_at, 0)
        many = counts[0] * counts[1]
        shaped = lambda w: w.reshape(many, 8, 128)
        *up2, shift2 = [shaped(all_tables[k]) for k in range(4)]
        ny = counts[1]
        y_z = lambda v: pair_sum(pair_sum(v, 1, 4), 2, 4)
        up3 = [
            y_z(take_odd(up2[0], 2, 1)),
            pair_sum(pair_sum(take_odd(up2[1], 1, 4), 2, 1), 2, 4),
            pair_sum(pair_sum(take_odd(up2[2], 2, 4), 2, 1), 1, 4),
        ]
        shift3 = pair_sum(y_z(shift2), 2, 1)
        fine = dense_tables(up2, shift2, 1, ny)
        coarse = dense_tables(up3, shift3, 2, ny)
        collect(side_at, 1)
        answer[...] = dense_cycle(shaped(all_side[...]), fine, coarse, ny)

    def answer_at(d, step):
        p = list(place)
        if d is not None:
            p[d] = lax.rem(p[d] + (counts[d] + step), counts[d])
        return local_of(answer[p[0] * counts[1] + p[1]], p[2])

    def corrected(halos, way):
        step = -1 if way == 0 else 1
        e = [answer_at(d, step) for d in range(3)]
        edge = lambda f, d: f.shape[d] - 1 if way == 0 else 0
        x, y, z = edge(e[0], 0), edge(e[1], 1), edge(e[2], 2)
        return [
            halos[0] + e[0][x],
            halos[1] + prolong(e[1][:, y : y + 1, :]),
            halos[2] + prolong(jnp.broadcast_to(e[2][:, :, z : z + 1], e[2].shape)),
        ]

    def exchange(v, meanwhile=None):
        r = count[0]
        count[0] += 1
        n = v.shape[0]
        plan = []
        for d in range(3):
            for way in range(2):
                at = v.shape[d] - 1 if way == 0 else 0
                if d == 0:
                    outs[0][r, way] = v[at]
                    src, dst = out_x.at[r, way], in_x.at[r, way]
                elif d == 1:
                    outs[1][r, way, pl.ds(0, n)] = v[:, at : at + 1, :]
                    src = out_y.at[r, way, pl.ds(0, n)]
                    dst = in_y.at[r, way, pl.ds(0, n)]
                else:
                    outs[2][r, way] = pack_z(v, at)
                    src, dst = out_z.at[r, way], in_z.at[r, way]
                k = 2 * d + way
                plan.append((src, dst, send_sem.at[r, k], recv_sem.at[r, k], d, way))
                send(*plan[-1])
        if meanwhile is not None:
            meanwhile()
        for item in plan:
            receive(*item)
        return [
            [in_x[r, way], in_y[r, way, pl.ds(0, n)], unpack_z(in_z[r, way], n)]
            for way in range(2)
        ]

    def inside(v, level):
        t, s = tables[level], 1 << level
        zero = [jnp.zeros(v.shape[1:], v.dtype), 0.0, 0.0]
        total = 0.0
        for d in range(3):
            total = total + (t[d] * up(v, zero, d, s) + t[3 + d] * down(v, zero, d, s))
        return total

    def outside(v, level, halos):
        low, high = halos
        t, s = tables[level], 1 << level
        total = 0.0
        for d in (1, 2):
            place_in = iota(v.shape, d)
            total = total + jnp.where(place_in >= v.shape[d] - s, t[d] * high[d], 0.0)
            total = total + jnp.where(place_in < s, t[3 + d] * low[d], 0.0)
        first, last = t[3, 0] * low[0], t[0, v.shape[0] - 1] * high[0]
        parts = [total[:1] + first[None], total[-1:] + last[None]]
        if v.shape[0] > 2:
            parts.insert(1, total[1:-1])
        return jnp.concatenate(parts, axis=0)

    def around(v, level, halos=None, meanwhile=None):
        if halos is None:
            box = []

            def work():
                if meanwhile is not None:
                    meanwhile()
                box.append(inside(v, level))

            halos = exchange(v, work)
            return box[0] + outside(v, level, halos)
        return inside(v, level) + outside(v, level, halos)

    def sweep(v, level, halos=None, meanwhile=None):
        t = tables[level]
        total = sides[level][...] + around(v, level, halos, meanwhile)
        return (1.0 - OMEGA) * v + t[7] * total

    def cycle(level):
        v = tables[level][7] * sides[level][...]
        if level == LEVELS - 1:
            for _ in range(COARSE_SWEEPS - 1):
                v = sweep(v, level)
            return v
        v = sweep(v, level, None, send_tables if gather and level == 0 else None)
        box = []
        halos = exchange(v, lambda: box.append(inside(v, level)))
        residual = sides[level][...] - tables[level][6] * v
        residual = residual + (box[0] + outside(v, level, halos))
        if gather and level == 1:
            coarse_solve(restrict(residual, 1 << level))
            v = v + prolong(answer_at(None, 0))
            v = sweep(v, level, [corrected(halos[0], 0), corrected(halos[1], 1)])
            return sweep(v, level)
        sides[level + 1][...] = restrict(residual, 1 << level)
        v = v + prolong(cycle(level + 1))
        for _ in range(2):
            v = sweep(v, level)
        return v

    stores = []
    pressure = cycle(0)
    low, high = exchange(pressure)
    change = jnp.zeros(shape, jnp.float32)
    fraction = frac_ref[...]
    for d in range(3):
        moved = open_u[d] - tables[0][d] * (up(pressure, high, d, 1) - pressure)
        moved_low = vel_low[d] - tables[0][3 + d] * (pressure - down(pressure, low, d, 1))
        out_velocity[d] = moved
        stores.append(
            pltpu.make_async_copy(out_velocity.at[d], vel_out.at[d], store_sem.at[d])
        )
        stores[-1].start()
        flux = moved * jnp.where(moved > 0, fraction, frac_up_ref[d])
        flux_low = moved_low * jnp.where(moved_low > 0, frac_down_ref[d], fraction)
        change = change + (flux - flux_low)
    out_fraction[...] = fraction - TIME_STEP * change
    stores.append(pltpu.make_async_copy(out_fraction, frac_out, store_sem.at[3]))
    stores[-1].start()

    for src, dst, ssem, rsem, d, way in sends:
        target = has_high[d] if way == 0 else has_low[d]

        @pl.when(target)
        def _():
            copy(src, dst, ssem, rsem, d, way).wait_send()

    for item in spreads:
        item.wait_send()
    for item in stores:
        item.wait()


def body(counts, kernel, *refs):
    (fill, flags, smear, velocity, vel_out, frac_out, *scratch) = refs
    loaded, scratch = scratch[:8], scratch[8:]
    first, scratch = scratch[:12], scratch[12:]
    tables, scratch = scratch[:LEVELS], scratch[LEVELS:]
    sides, scratch = scratch[:LEVELS], scratch[LEVELS:]
    kernel(
        counts, fill, flags, smear, velocity, vel_out, frac_out, *loaded,
        *first, tables, sides, *scratch,
    )


def shards(counts, fill_mask, membrane_flags, smear, velocity):
    nx, ny, nz = fill_mask.shape
    f32 = jnp.float32
    vmem = lambda *s: pltpu.VMEM(s, f32)
    first = [vmem(2, 3, ny, nz), vmem(2, 3, nx, 1, nz), vmem(2, 3, ny, nz)] * 2
    many = 8 if gathers(counts, fill_mask.shape) else ROUNDS
    rounds = [vmem(many, 2, ny, nz), vmem(many, 2, nx, 1, nz), vmem(many, 2, ny, nz)] * 2
    tables = [vmem(8, nx >> l, ny, nz) for l in range(LEVELS)]
    sides = [vmem(nx >> l, ny, nz) for l in range(LEVELS)]
    rest = [vmem(3, nx, ny, nz), vmem(3, nx, ny, nz), vmem(nx, ny, nz)]
    rest += [vmem(3, nx, ny, nz), vmem(3, nx, ny, nz)]
    sems = [pltpu.SemaphoreType.DMA((6,))] * 2 + [pltpu.SemaphoreType.DMA((many, 6))] * 2
    loaded = [pltpu.VMEM(a.shape, a.dtype) for a in (fill_mask, membrane_flags, smear, velocity)]
    loaded += [pltpu.SemaphoreType.DMA((4,))]
    loaded += [vmem(*velocity.shape), vmem(*fill_mask.shape), pltpu.SemaphoreType.DMA((4,))]
    many = counts[0] * counts[1]
    peers = many * counts[2] if gathers(counts, fill_mask.shape) else 1
    sems += [
        vmem(4, 2, 1, nz), vmem(4, many, 2, counts[2], 1, nz), vmem(2, 1, nz),
        vmem(many, 2, counts[2], 1, nz), vmem(many, ny, nz),
    ] + [pltpu.SemaphoreType.DMA((2, peers))] * 2
    whole = pl.BlockSpec(memory_space=pltpu.VMEM)
    left = pl.BlockSpec(memory_space=pl.ANY)
    return pl.pallas_call(
        functools.partial(body, counts, kernel),
        out_shape=(
            jax.ShapeDtypeStruct(velocity.shape, f32),
            jax.ShapeDtypeStruct(fill_mask.shape, f32),
        ),
        in_specs=[left] * 4,
        out_specs=(left, left),
        scratch_shapes=loaded + first + rounds + tables + sides + rest + sems,
        compiler_params=pltpu.CompilerParams(
            collective_id=0, has_side_effects=True, vmem_limit_bytes=60 * 1024 * 1024
        ),
    )(fill_mask, membrane_flags, smear, velocity)


def solution(mesh):
    placed = (P("gx", "gy", "gz"),) * 3 + (P(None, "gx", "gy", "gz"),)
    counts = tuple(mesh.shape[a] for a in AXES)
    return jax.shard_map(
        functools.partial(shards, counts),
        mesh=mesh,
        in_specs=placed,
        out_specs=(P(None, "gx", "gy", "gz"), P("gx", "gy", "gz")),
        check_vma=False,
    )
```
